32 devices in a mesh: batch: 2 (over core), seq: 16 (over z, y, x).
Axes of the slice: x: 2, y: 2, z: 4, core: 2. Of those that a mesh axis runs over, the one named last changes fastest.
Arguments:
- tokens: bfloat16 [2, 4096, 768], P('batch', 'seq'), may hold values from -6 to 6
- w_query: bfloat16 [768, 768], replicated, may hold values from -0.21875 to 0.21875
- w_key: bfloat16 [768, 768], replicated, may hold values from -0.21875 to 0.21875
- w_value: bfloat16 [768, 768], replicated, may hold values from -0.21875 to 0.21875
- w_out: bfloat16 [768, 768], replicated, may hold values from -0.3125 to 0.3125
- w_up: bfloat16 [768, 3072], replicated, may hold values from -0.21875 to 0.21875
- w_down: bfloat16 [3072, 768], replicated, may hold values from -0.15625 to 0.15625
- gain_mix: float32 [768], replicated, may hold values from 0.5 to 1.5
- gain_ffn: float32 [768], replicated, may hold values from 0.5 to 1.5
- taps: float32 [4, 768], replicated, may hold values from -3 to 3
- rate: float32 [64, 768], replicated, may hold values from 4.8828125e-05 to 0.03125, as said below
- gain_b: float32 [64, 768], replicated, may hold values from -4 to 4
- gain_c: float32 [64, 768], replicated, may hold values from -1 to 1
- skip: float32 [768], replicated, may hold values from -4 to 4
- cotangent: bfloat16 [2, 4096, 768], P('batch', 'seq'), may hold values from -6 to 6
Outputs:
- output: bfloat16 [2, 4096, 768], P('batch', 'seq')
- d_tokens: bfloat16 [2, 4096, 768], P('batch', 'seq')
- d_query: float32 [768, 768], replicated
- d_key: float32 [768, 768], replicated
- d_value: float32 [768, 768], replicated
- d_out: float32 [768, 768], replicated
- d_up: float32 [768, 3072], replicated
- d_down: float32 [3072, 768], replicated
- d_gain_mix: float32 [768], replicated
- d_gain_ffn: float32 [768], replicated
- d_taps: float32 [4, 768], replicated
- d_rate: float32 [64, 768], replicated
- d_gain_b: float32 [64, 768], replicated
- d_gain_c: float32 [64, 768], replicated
- d_skip: float32 [768], replicated
The draws below stay inside these ranges and needn't reach their ends.
Inputs may be any that keep to these rules, and one draw needn't show every extreme that they name: Every rate is positive.
All inputs are finite; a program needn't handle non-finite values.
Results may differ from the reference program's by a relative error of at most 0.0095.
Values sent between devices are 32-bit elements; how exact they have to be, the bound alone decides.
No kernel may reach another device: no remote copies, remote signals or barrier semaphores. Data moves between devices by JAX's collectives and lax.ppermute only.
A program may use at most 256 MiB of HBM per device.

```python
import math
import jax
import jax.numpy as jnp
from jax import lax

D = 768
FF = 3072
NS = 64
TAPS = 4
TOK_DEV = 256
LEN = 4096
SEQS = 2


def draw_rate(key, part):
    picker, spread = jax.random.split(jax.random.fold_in(key, 11))
    share = 0.5
    slowest = math.log(0.2 / LEN)
    middle = math.log(2.0 / LEN)
    fastest = math.log(1.0 / 32)
    slow_flag = jax.random.uniform(picker, (NS, D), jnp.float32) < share
    where = jax.random.uniform(spread, (NS, D), jnp.float32)
    slow_rate = jnp.exp(slowest + where * (middle - slowest))
    fast_rate = jnp.exp(middle + where * (fastest - middle))
    return jnp.where(slow_flag, slow_rate, fast_rate).astype(jnp.float32)


def block_levels(key, dims, cuts, low, high):
    loudness, own = 1.0, jax.random.fold_in(key, 6)
    for dim, parts in cuts:
        heights = jnp.exp(jax.random.uniform(jax.random.fold_in(own, dim), (parts,), jnp.float32, low / len(cuts), high / len(cuts)))
        loudness = loudness * jnp.repeat(heights, dims[dim] // parts).reshape([-1 if axis == dim else 1 for axis in range(len(dims))])
    return loudness


def scatter_about(stream_key, extent, scale, most, pieces=(), held_as=jnp.bfloat16):
    values = scale * jax.random.normal(stream_key, extent, jnp.float32)
    if pieces:
        values = values * block_levels(stream_key, extent, pieces, -0.22, 0.18)
    return jnp.clip(values, -most, most).astype(held_as)


def setup_inputs(seed: int = 0) -> dict:
    keys = jax.random.split(jax.random.key(seed), 16)
    tokens = scatter_about(keys[0], (SEQS, LEN, D), 1.0, 6.0, ((0, 2), (1, 16)))
    w_query = scatter_about(keys[1], (D, D), D ** -0.5, 0.21875)
    w_key = scatter_about(keys[2], (D, D), D ** -0.5, 0.21875)
    w_value = scatter_about(keys[3], (D, D), D ** -0.5, 0.21875)
    w_out = scatter_about(keys[4], (D, D), (D // 2) ** -0.5, 0.3125)
    w_up = scatter_about(keys[5], (D, FF), D ** -0.5, 0.21875)
    w_down = scatter_about(keys[6], (FF, D), (FF // 2) ** -0.5, 0.15625)
    gain_mix = jnp.clip(1.0 + 0.1 * jax.random.normal(keys[7], (D,), jnp.float32), 0.5, 1.5)
    gain_ffn = jnp.clip(1.0 + 0.1 * jax.random.normal(keys[8], (D,), jnp.float32), 0.5, 1.5)
    taps = scatter_about(keys[9], (TAPS, D), 0.6, 3.0, (), jnp.float32)
    rate = draw_rate(jax.random.fold_in(keys[15], 71), 0)
    gain_b = scatter_about(keys[11], (NS, D), 1.0, 4.0, (), jnp.float32)
    gain_c = scatter_about(keys[12], (NS, D), (NS // 2) ** -0.5, 1.0, (), jnp.float32)
    skip = scatter_about(keys[13], (D,), 1.0, 4.0, (), jnp.float32)
    cotangent = scatter_about(keys[14], (SEQS, LEN, D), 1.0, 6.0, ((0, 2), (1, 16)))
    return {"tokens": tokens, "w_query": w_query, "w_key": w_key, "w_value": w_value, "w_out": w_out, "w_up": w_up, "w_down": w_down, "gain_mix": gain_mix, "gain_ffn": gain_ffn, "taps": taps, "rate": rate, "gain_b": gain_b, "gain_c": gain_c, "skip": skip, "cotangent": cotangent}


@jax.custom_vjp
def low(v):
    return lax.optimization_barrier(v.astype(jnp.bfloat16)).astype(jnp.float32)

@jax.custom_vjp
def low_back(v):
    return v

def low_keep(v):
    return (low(v), None)

def low_pass(kept, grad):
    return (grad,)

def back_keep(v):
    return (v, None)

def back_low(kept, grad):
    return (low(grad),)
low.defvjp(low_keep, low_pass)
low_back.defvjp(back_keep, back_low)
HIGHEST = lax.Precision.HIGHEST

def block_powers(rate, count):
    steps = jnp.arange(count).astype(jnp.float32)
    return jnp.exp(-steps[:, None, None] * rate[None])

def lower_toeplitz(kernel):
    length = kernel.shape[0]
    padded = jnp.concatenate([kernel[:1], jnp.zeros_like(kernel), jnp.flip(kernel[1:], 0)], 0)
    tiled = jnp.tile(padded, (length, 1))[:length * (2 * length - 1)]
    return tiled.reshape(length, 2 * length - 1, kernel.shape[1])[:, :length]

def combine(earlier, later):
    return (earlier[0] * later[0], earlier[1] * later[0] + later[1])

def local_part(inputs, rate, gain_b, gain_c, skip):
    rows, width = inputs.shape
    length = min(16, rows)
    number = rows // length
    scale = gain_b * jnp.sqrt(-jnp.expm1(-2.0 * rate))
    powers = block_powers(rate, length + 1)
    kernel = jnp.einsum('jnc,nc->jc', powers[:length], gain_c * scale, precision=HIGHEST)
    toeplitz = lower_toeplitz(kernel)
    blocks = inputs.reshape(number, length, width)
    inner = jnp.einsum('tsc,isc->itc', toeplitz, blocks, precision=HIGHEST)
    ends = jnp.einsum('snc,isc->inc', jnp.flip(powers[:length], 0), blocks, precision=HIGHEST) * scale
    factor = jnp.broadcast_to(powers[length], ends.shape)
    states = lax.associative_scan(combine, (factor, ends), axis=0)[1]
    return (inner.reshape(rows, width) + skip * inputs, states)

def with_entry(direct, states, entering, rate, gain_c):
    rows, width = direct.shape
    number = states.shape[0]
    length = rows // number
    powers = block_powers(rate, length + 1)
    entry = block_powers(rate * length, number + 1)
    starts = jnp.concatenate([jnp.zeros_like(states[:1]), states[:-1]], 0) + entry[:number] * entering[None]
    carried = jnp.einsum('tnc,inc->itc', powers[1:], starts * gain_c, precision=HIGHEST)
    return (direct + carried.reshape(rows, width), states[-1] + entry[number] * entering)

def mixer(inputs, entering, rate, gain_b, gain_c, skip):
    direct, states = local_part(inputs, rate, gain_b, gain_c, skip)
    return with_entry(direct, states, entering, rate, gain_c)

def layer_norm(rows_in, gain):
    centred = rows_in - lax.optimization_barrier(jnp.mean(rows_in, -1, keepdims=True))
    spread = lax.optimization_barrier(jnp.mean(centred * centred, -1, keepdims=True))
    return centred * lax.rsqrt(spread + 1e-05) * gain

def matmul(left, right):
    return jnp.dot(left, right, precision=HIGHEST)

def layer(sequence, w_query, w_key, w_value, w_out, w_up, w_down, gain_mix, gain_ffn, taps, rate, gain_b, gain_c, skip):
    length, width = sequence.shape
    mixed_in = low(layer_norm(sequence, gain_mix))
    queries = low_back(matmul(mixed_in, w_query))
    key_rows = low_back(matmul(mixed_in, w_key))
    values = low_back(matmul(mixed_in, w_value))
    padded = jnp.concatenate([jnp.zeros((3, width), jnp.float32), key_rows], 0)
    shifted = taps[0] * padded[3:] + taps[1] * padded[2:-1] + taps[2] * padded[1:-2] + taps[3] * padded[:-3]
    inputs = shifted * values
    state_size = rate.shape[0]

    def run(carry, block):
        mixed_block, carry_next = jax.checkpoint(mixer)(block, carry, rate, gain_b, gain_c, skip)
        return (carry_next, mixed_block)
    blocks = inputs.reshape(length // TOK_DEV, TOK_DEV, width)
    mixed = lax.scan(run, jnp.zeros((state_size, width), jnp.float32), blocks)[1].reshape(length, width)
    gated = low(queries * mixed)
    hidden = sequence + low_back(matmul(gated, w_out))
    ffn_in = low(layer_norm(hidden, gain_ffn))
    upper = low_back(matmul(ffn_in, w_up))
    act = low(jax.nn.gelu(upper, approximate=True))
    return hidden + low_back(matmul(act, w_down))

def reference(tokens, w_query, w_key, w_value, w_out, w_up, w_down, gain_mix, gain_ffn, taps, rate, gain_b, gain_c, skip, cotangent):
    params = tuple((w.astype(jnp.float32) for w in (w_query, w_key, w_value, w_out, w_up, w_down)))
    params = params + (gain_mix, gain_ffn, taps, rate, gain_b, gain_c, skip)

    def one(totals, pair):
        sequence, cot_seq = pair
        result, pullback = jax.vjp(layer, sequence.astype(jnp.float32), *params)
        grads = pullback(cot_seq.astype(jnp.float32))
        totals = jax.tree.map(jnp.add, totals, tuple(grads[1:]))
        return (totals, (result.astype(jnp.bfloat16), grads[0].astype(jnp.bfloat16)))
    zeros = tuple((jnp.zeros_like(p) for p in params))
    totals, (outputs, d_inputs) = lax.scan(one, zeros, (tokens, cotangent))
    return (outputs, d_inputs) + totals
```

```python
import jax
import jax.numpy as jnp
from jax import lax
from jax.experimental import pallas as pl
from jax.experimental.pallas import tpu as pltpu
from jax.sharding import PartitionSpec as P

F32 = jnp.float32
BF16 = jnp.bfloat16
LANES = 128


def cost(flops, moved):
    return pl.CostEstimate(flops=flops, bytes_accessed=moved, transcendentals=0)


def col_spec(rows):
    return pl.BlockSpec((rows, LANES), lambda g: (0, g))


def per_group(kernel, ins, outs, scratch, flops):
    width = ins[0].shape[1]
    moved = sum(x.size * x.dtype.itemsize for x in ins) + sum(
        rows * width * jnp.dtype(kind).itemsize for rows, kind in outs
    )
    return pl.pallas_call(
        kernel,
        grid=(width // LANES,),
        in_specs=[col_spec(x.shape[0]) for x in ins],
        out_specs=[col_spec(rows) for rows, _ in outs],
        out_shape=[jax.ShapeDtypeStruct((rows, width), kind) for rows, kind in outs],
        scratch_shapes=scratch,
        cost_estimate=cost(flops, moved),
        compiler_params=pltpu.CompilerParams(vmem_limit_bytes=32 * 1024 * 1024),
    )(*ins)


def folded(product):
    return jnp.sum(product.reshape(product.shape[0] // 8, 8, product.shape[1]), 0)


def unfold(parts_ref, rows):
    total = parts_ref[pl.ds(0, rows, stride=8), :]
    for s in range(1, 8):
        total = total + parts_ref[pl.ds(s, rows, stride=8), :]
    return total


def ends_kernel(key_ref, value_ref, rim_ref, taps_ref, rate_ref, shifted_ref, inputs_ref, end_ref, pad):
    rows = key_ref.shape[0]
    pad[0:8, :] = rim_ref[...]
    pad[8:, :] = key_ref[...]
    shifted = taps_ref[0:1, :] * pad[8:, :]
    for j in range(1, 4):
        shifted = shifted + taps_ref[j : j + 1, :] * pad[8 - j : 8 - j + rows, :]
    shifted_ref[...] = shifted
    inputs_ref[...] = shifted * value_ref[...]
    decay = jnp.exp(-rate_ref[...])

    def lap(i, state):
        for k in range(16):
            state = decay * state + inputs_ref[pl.ds(i * 16 + k, 1), :]
        return state

    end_ref[...] = lax.fori_loop(0, rows // 16, lap, jnp.zeros_like(decay))


def mix_kernel(
    inputs_ref, query_ref, enter_ref, rate_ref, read_ref, skip_ref, mixed_ref, gated_ref, parts
):
    rows = inputs_ref.shape[0]
    decay = jnp.exp(-rate_ref[...])
    read = read_ref[...]

    def lap(i, state):
        for k in range(16):
            t = i * 16 + k
            state = decay * state + inputs_ref[pl.ds(t, 1), :]
            parts[pl.ds(pl.multiple_of(t * 8, 8), 8), :] = folded(read * state)
        return state

    lax.fori_loop(0, rows // 16, lap, enter_ref[...])
    mixed = unfold(parts, rows) + skip_ref[...] * inputs_ref[...]
    mixed_ref[...] = mixed
    gated_ref[...] = (query_ref[...] * mixed).astype(BF16)


def towards_kernel(
    grad_ref, query_ref, mixed_ref, rate_ref, grad_query_ref, grad_mixed_ref, start_ref
):
    rows = grad_ref.shape[0]
    grad_query_ref[...] = (grad_ref[...] * mixed_ref[...]).astype(BF16)
    grad_mixed_ref[...] = grad_ref[...] * query_ref[...]
    decay = jnp.exp(-rate_ref[...])

    def lap(i, state):
        for k in range(16):
            state = decay * state + grad_mixed_ref[pl.ds(rows - 1 - i * 16 - k, 1), :]
        return state

    start_ref[...] = lax.fori_loop(0, rows // 16, lap, jnp.zeros_like(decay))


def back_kernel(
    grad_ref,
    inputs_ref,
    shifted_ref,
    value_ref,
    key_ref,
    rim_ref,
    taps_ref,
    rate_ref,
    read_ref,
    skip_ref,
    enter_ref,
    adjoint_ref,
    grad_value_ref,
    grad_key_ref,
    head_ref,
    sum_ref,
    slope_ref,
    small_ref,
    parts,
    pad,
):
    rows = grad_ref.shape[0]
    decay = jnp.exp(-rate_ref[...])
    read = read_ref[...]
    zero = jnp.zeros_like(decay)

    def lap(i, carry):
        adjoint, ramp, total, slope = carry
        for k in range(8):
            t = rows - 1 - i * 8 - k
            entry = inputs_ref[pl.ds(t, 1), :]
            slope = slope + entry * ramp
            adjoint = decay * adjoint + grad_ref[pl.ds(t, 1), :]
            total = total + entry * adjoint
            parts[pl.ds(pl.multiple_of(t * 8, 8), 8), :] = folded(read * adjoint)
            ramp = decay * ramp + adjoint
        return adjoint, ramp, total, slope

    _, ramp, total, slope = lax.fori_loop(
        0, rows // 8, lap, (adjoint_ref[...], zero, zero, zero)
    )
    sum_ref[...] = total
    slope_ref[...] = slope + enter_ref[...] * ramp
    grad = grad_ref[...]
    grad_inputs = unfold(parts, rows) + skip_ref[...] * grad
    grad_value_ref[...] = (grad_inputs * shifted_ref[...]).astype(BF16)
    grad_shifted = grad_inputs * value_ref[...]
    pad[0:rows, :] = grad_shifted
    pad[rows:, :] = jnp.zeros_like(head_ref)
    head_ref[...] = pad[0:8, :]
    grad_key = taps_ref[0:1, :] * grad_shifted
    for j in range(1, 4):
        grad_key = grad_key + taps_ref[j : j + 1, :] * pad[j : j + rows, :]
    grad_key_ref[...] = grad_key
    pad[0:8, :] = rim_ref[...]
    pad[8:, :] = key_ref[...]
    small = [
        jnp.sum(grad_shifted * pad[8 - j : 8 - j + rows, :], 0, keepdims=True) for j in range(4)
    ]
    small.append(jnp.sum(grad * inputs_ref[...], 0, keepdims=True))
    small.append(jnp.zeros((3, LANES), F32))
    small_ref[...] = jnp.concatenate(small, 0)


def bits_of(count):
    out, step = [], 1
    while step < count:
        out.append(step)
        step *= 2
    return out


class Wires:
    def __init__(self):
        self.batch, self.seq = lax.axis_size("batch"), lax.axis_size("seq")
        bits = bits_of(self.seq)
        self.orders = (tuple(bits), tuple(bits[1::-1] + bits[2:]))
        self.spare = bits_of(self.batch)[1:]
        self.core = lax.axis_index("batch") % 2
        self.place = lax.axis_index("seq")
        self.steps = len(bits)

    def bit(self, step, core=None):
        core = self.core if core is None else core
        first, second = ((self.place // order[step]) % 2 for order in self.orders)
        return jnp.where(core == 0, first, second)

    def swap(self, value, step):
        pairs = [
            (b * self.seq + s, b * self.seq + (s ^ self.orders[b % 2][step]))
            for b in range(self.batch)
            for s in range(self.seq)
        ]
        return lax.ppermute(value, ("batch", "seq"), pairs)

    def swap_batch(self, value, step):
        return lax.ppermute(value, "batch", [(b, b ^ step) for b in range(self.batch)])

    def scatter_sum(self, send, keep):
        keep_in, received = keep, self.swap_batch(send, 1)
        for step in range(self.steps):
            mine = self.bit(step)
            send = half(keep_in, 1 - mine) + half(received, 1 - mine)
            arriving = self.swap(send, step)
            keep_in = half(keep_in, mine) + half(received, mine)
            received = arriving
        total = keep_in + received
        for step in self.spare:
            total = total + self.swap_batch(total, step)
        return total

    def gather(self, block):
        for step in range(self.steps - 1, 0, -1):
            mine = self.bit(step) == 0
            arriving = self.swap(block, step)
            block = jnp.concatenate(
                [jnp.where(mine, block, arriving), jnp.where(mine, arriving, block)], 0
            )
        other = self.swap(block, 0)
        return block, other, self.swap_batch(block, 1), self.swap_batch(other, 1)

    def halves(self, quarters):
        own, other, far, far_other = quarters
        mine = self.bit(0) == 0
        theirs = self.bit(0, 1 - self.core) == 0
        first = self.core == 0
        here = (jnp.where(mine, own, other), jnp.where(mine, other, own))
        there = (jnp.where(theirs, far, far_other), jnp.where(theirs, far_other, far))
        return [
            jnp.concatenate([jnp.where(first, h, t) for h, t in zip(here, there)], 0),
            jnp.concatenate([jnp.where(first, t, h) for h, t in zip(here, there)], 0),
        ]


def half(value, which):
    rows = value.shape[0] // 2
    return lax.dynamic_slice_in_dim(value, which * rows, rows, 0)


def prefix(ends, rate, rows, backward):
    count = lax.axis_size("seq")
    place = lax.axis_index("seq")
    rank = count - 1 - place if backward else place
    total = ends
    entering = jnp.zeros_like(ends)
    steps = bits_of(count)
    for step in steps:
        arriving = lax.ppermute(total, "seq", [(s, s ^ step) for s in range(count)])
        upper = (rank // step) % 2 == 1
        behind = ((rank % step) * rows).astype(F32)
        entering = jnp.where(upper, entering + jnp.exp(-rate * behind) * arriving, entering)
        if step != steps[-1]:
            early = jnp.where(upper, arriving, total)
            late = jnp.where(upper, total, arriving)
            total = jnp.exp(-rate * (step * rows)) * early + late
    return entering


def layer_norm(rows_in, gain):
    centred = rows_in - jnp.mean(rows_in, -1, keepdims=True)
    spread = jnp.mean(centred * centred, -1, keepdims=True)
    return centred * lax.rsqrt(spread + 1e-05) * gain


def gelu_tanh(upper):
    return jax.nn.gelu(upper, approximate=True)


def product(left, right):
    return jnp.dot(left, right, preferred_element_type=F32)


def weight_grad(left, right):
    return jnp.einsum("ti,tj->ij", left, right, preferred_element_type=F32)


def back_product(grad_rows, weight):
    return jnp.einsum("tj,ij->ti", grad_rows, weight, preferred_element_type=F32)


def local(
    tokens,
    w_query,
    w_key,
    w_value,
    w_out,
    w_up,
    w_down,
    gain_mix,
    gain_ffn,
    taps,
    rate,
    gain_b,
    gain_c,
    skip,
    cotangent,
):
    _, rows, width = tokens.shape
    count = lax.axis_size("seq")
    states = rate.shape[0]
    wires = Wires()
    skip_row = skip.reshape(1, width)
    scale = gain_b * jnp.sqrt(-jnp.expm1(-2.0 * rate))
    read = gain_c * scale

    flat_in = tokens.astype(F32).reshape(rows, width)
    normed, norm_pull = jax.vjp(layer_norm, flat_in, gain_mix)
    mixed_in = normed.astype(BF16)
    rim_own = product(layer_norm(flat_in[rows - 8 :], gain_mix).astype(BF16), w_key)
    rim = lax.ppermute(rim_own, "seq", [(s, s + 1) for s in range(count - 1)])
    queries = product(mixed_in, w_query)
    key_rows = product(mixed_in, w_key)
    values = product(mixed_in, w_value)
    element = rows * states * width
    shifted, inputs, ends = per_group(
        ends_kernel,
        (key_rows, values, rim, taps, rate),
        ((rows, F32), (rows, F32), (states, F32)),
        [pltpu.VMEM((rows + 8, LANES), F32)],
        2 * element,
    )
    entering = prefix(ends, rate, rows, False)
    mixed, gated = per_group(
        mix_kernel,
        (inputs, queries, entering, rate, read, skip_row),
        ((rows, F32), (rows, BF16)),
        [pltpu.VMEM((rows * 8, LANES), F32)],
        4 * element,
    )
    hidden = flat_in + product(gated, w_out)
    ffn_normed, ffn_pull = jax.vjp(layer_norm, hidden, gain_ffn)
    ffn_in = ffn_normed.astype(BF16)
    upper = product(ffn_in, w_up)
    activated, gelu_pull = jax.vjp(gelu_tanh, upper)
    act = activated.astype(BF16)
    grad_out = cotangent.reshape(rows, width)

    def by_columns(left, right):
        return (
            weight_grad(half_columns(left, 1 - wires.core), right),
            weight_grad(half_columns(left, wires.core), right),
        )

    def by_tensor(first, second):
        picked = [jnp.where(wires.core == 0, a, b) for a, b in zip(first, second)]
        others = [jnp.where(wires.core == 0, b, a) for a, b in zip(first, second)]
        return weight_grad(*others), weight_grad(*picked)

    middle = act.shape[1] // 2
    chunks = []
    chunks.append(wires.scatter_sum(*by_columns(act[:, :middle], grad_out)))
    chunks.append(wires.scatter_sum(*by_columns(act[:, middle:], grad_out)))
    grad_act = back_product(grad_out, w_down)
    grad_upper = gelu_pull(grad_act)[0].astype(BF16)
    chunks.append(wires.scatter_sum(*by_columns(ffn_in[:, : width // 2], grad_upper)))
    chunks.append(wires.scatter_sum(*by_columns(ffn_in[:, width // 2 :], grad_upper)))
    output = hidden + product(act, w_down)
    grad_ffn = back_product(grad_upper, w_up)
    grad_hidden_norm, d_gain_ffn = ffn_pull(grad_ffn)
    grad_hidden = grad_out.astype(F32) + grad_hidden_norm
    grad_branch = grad_hidden.astype(BF16)
    grad_gated = back_product(grad_branch, w_out)
    grad_queries, grad_mixed, starts = per_group(
        towards_kernel,
        (grad_gated, queries, mixed, rate),
        ((rows, BF16), (rows, F32), (states, F32)),
        [],
        2 * element,
    )
    chunks.append(wires.scatter_sum(*by_tensor((gated, grad_branch), (mixed_in, grad_queries))))
    adjoint = prefix(starts, rate, rows, True)
    grad_values, grad_keys_local, head, sums, slopes, small = per_group(
        back_kernel,
        (
            grad_mixed,
            inputs,
            shifted,
            values,
            key_rows,
            rim,
            taps,
            rate,
            read,
            skip_row,
            entering,
            adjoint,
        ),
        ((rows, BF16), (rows, F32), (8, F32), (states, F32), (states, F32), (8, F32)),
        [pltpu.VMEM((rows * 8, LANES), F32), pltpu.VMEM((rows + 8, LANES), F32)],
        10 * element,
    )
    behind = lax.ppermute(head, "seq", [(s + 1, s) for s in range(count - 1)])
    padded = jnp.concatenate([jnp.zeros_like(behind), behind[:4]], 0)
    late = sum(taps[j] * padded[j : j + 8] for j in range(1, 4))
    grad_keys = jnp.concatenate(
        [grad_keys_local[: rows - 8], grad_keys_local[rows - 8 :] + late], 0
    ).astype(BF16)
    chunks.append(wires.scatter_sum(*by_tensor((mixed_in, grad_keys), (mixed_in, grad_values))))
    grad_normed = (
        back_product(grad_queries, w_query)
        + back_product(grad_keys, w_key)
        + back_product(grad_values, w_value)
    )
    grad_input_norm, d_gain_mix = norm_pull(grad_normed)
    d_tokens = (grad_hidden + grad_input_norm).astype(BF16).reshape(tokens.shape)

    extra = max(64, states - (-states) % 64)
    extra = 2 * extra
    filler = jnp.zeros((extra - states - 5, width), F32)
    few = jnp.zeros((extra - states - 2, width), F32)
    part_a = jnp.concatenate([sums, small[:5], filler], 0)
    part_b = jnp.concatenate([slopes, d_gain_mix[None], d_gain_ffn[None], few], 0)
    chunks.append(
        wires.scatter_sum(
            jnp.where(wires.core == 0, part_b, part_a), jnp.where(wires.core == 0, part_a, part_b)
        )
    )
    whole = [wires.halves(wires.gather(chunk)) for chunk in chunks]
    d_down = jnp.concatenate(whole[0] + whole[1], 0)
    d_up = jnp.concatenate(whole[2] + whole[3], 0)
    d_out, d_query = whole[4]
    d_key, d_value = whole[5]
    part_a, part_b = whole[6]
    sums, slopes = part_a[:states], part_b[:states]
    d_scale = gain_c * sums
    d_decay = read * slopes
    root = jnp.sqrt(-jnp.expm1(-2.0 * rate))
    d_rate = -jnp.exp(-rate) * d_decay + d_scale * gain_b * jnp.exp(-2.0 * rate) / root
    return (
        output.astype(BF16).reshape(tokens.shape),
        d_tokens,
        d_query,
        d_key,
        d_value,
        d_out,
        d_up,
        d_down,
        part_b[states],
        part_b[states + 1],
        part_a[states : states + 4],
        d_rate,
        d_scale * root,
        scale * sums,
        part_a[states + 4],
    )


def half_columns(value, which):
    columns = value.shape[1] // 2
    return lax.dynamic_slice_in_dim(value, which * columns, columns, 1)


def solution(mesh):
    split = P("batch", "seq", None)
    in_specs = (split,) + (P(),) * 13 + (split,)
    out_specs = (split, split) + (P(),) * 13
    return jax.shard_map(local, mesh=mesh, in_specs=in_specs, out_specs=out_specs, check_vma=False)
```

```python
import jax
import jax.numpy as jnp
from jax import lax
from jax.experimental import pallas as pl
from jax.experimental.pallas import tpu as pltpu
from jax.sharding import PartitionSpec as P

F32 = jnp.float32
BF16 = jnp.bfloat16
LANES = 128


def cost(micros):
    return pl.CostEstimate(flops=0, bytes_accessed=int(micros * 3.4e6), transcendentals=0)


def col_spec(rows):
    return pl.BlockSpec((rows, LANES), lambda g: (0, g))


def per_group(kernel, ins, outs, scratch, micros):
    width = ins[0].shape[1]
    return pl.pallas_call(
        kernel,
        grid=(width // LANES,),
        in_specs=[col_spec(x.shape[0]) for x in ins],
        out_specs=[col_spec(rows) for rows, _ in outs],
        out_shape=[jax.ShapeDtypeStruct((rows, width), kind) for rows, kind in outs],
        scratch_shapes=scratch,
        cost_estimate=cost(micros),
        compiler_params=pltpu.CompilerParams(vmem_limit_bytes=32 * 1024 * 1024),
    )(*ins)


def folded(product):
    return jnp.sum(product.reshape(product.shape[0] // 8, 8, product.shape[1]), 0)


def unfold(parts_ref, rows):
    total = parts_ref[pl.ds(0, rows, stride=8), :]
    for s in range(1, 8):
        total = total + parts_ref[pl.ds(s, rows, stride=8), :]
    return total


def both_kernel(own_ref, far_ref, out_ref):
    rows = own_ref.shape[0]
    out_ref[0:rows, :] = own_ref[...]
    out_ref[rows:, :] = far_ref[...].astype(BF16)


def both(own, far):
    rows, width = own.shape
    block = 3 * LANES
    return pl.pallas_call(
        both_kernel,
        grid=(width // block,),
        in_specs=[pl.BlockSpec((rows, block), lambda g: (0, g))] * 2,
        out_specs=pl.BlockSpec((2 * rows, block), lambda g: (0, g)),
        out_shape=jax.ShapeDtypeStruct((2 * rows, width), BF16),
        cost_estimate=cost(rows * width * 10 / 3.4e6),
    )(own, far)


def ends_kernel(key_ref, value_ref, rim_ref, taps_ref, rate_ref, shifted_ref, inputs_ref, end_ref, pad):
    rows = key_ref.shape[0]
    pad[0:8, :] = rim_ref[...]
    pad[8:, :] = key_ref[...]
    shifted = taps_ref[0:1, :] * pad[8:, :]
    for j in range(1, 4):
        shifted = shifted + taps_ref[j : j + 1, :] * pad[8 - j : 8 - j + rows, :]
    shifted_ref[...] = shifted
    inputs_ref[...] = shifted * value_ref[...]
    decay = jnp.exp(-rate_ref[...])

    def lap(i, state):
        for k in range(16):
            state = decay * state + inputs_ref[pl.ds(i * 16 + k, 1), :]
        return state

    end_ref[...] = lax.fori_loop(0, rows // 16, lap, jnp.zeros_like(decay))


def mix_kernel(
    inputs_ref, query_ref, enter_ref, rate_ref, read_ref, skip_ref, mixed_ref, gated_ref, parts
):
    rows = inputs_ref.shape[0]
    decay = jnp.exp(-rate_ref[...])
    read = read_ref[...]

    def lap(i, state):
        for k in range(16):
            t = i * 16 + k
            state = decay * state + inputs_ref[pl.ds(t, 1), :]
            parts[pl.ds(pl.multiple_of(t * 8, 8), 8), :] = folded(read * state)
        return state

    lax.fori_loop(0, rows // 16, lap, enter_ref[...])
    mixed = unfold(parts, rows) + skip_ref[...] * inputs_ref[...]
    mixed_ref[...] = mixed
    gated_ref[...] = (query_ref[...] * mixed).astype(BF16)


def towards_kernel(
    grad_ref, query_ref, mixed_ref, rate_ref, grad_query_ref, grad_mixed_ref, start_ref
):
    rows = grad_ref.shape[0]
    grad_query_ref[...] = (grad_ref[...] * mixed_ref[...]).astype(BF16)
    grad_mixed_ref[...] = grad_ref[...] * query_ref[...]
    decay = jnp.exp(-rate_ref[...])

    def lap(i, state):
        for k in range(16):
            state = decay * state + grad_mixed_ref[pl.ds(rows - 1 - i * 16 - k, 1), :]
        return state

    start_ref[...] = lax.fori_loop(0, rows // 16, lap, jnp.zeros_like(decay))


def back_kernel(
    grad_ref,
    inputs_ref,
    shifted_ref,
    value_ref,
    key_ref,
    rim_ref,
    taps_ref,
    rate_ref,
    read_ref,
    skip_ref,
    enter_ref,
    adjoint_ref,
    grad_value_ref,
    grad_key_ref,
    head_ref,
    sum_ref,
    slope_ref,
    small_ref,
    parts,
    pad,
):
    rows = grad_ref.shape[0]
    decay = jnp.exp(-rate_ref[...])
    read = read_ref[...]
    zero = jnp.zeros_like(decay)

    def lap(i, carry):
        adjoint, ramp, total, slope = carry
        for k in range(8):
            t = rows - 1 - i * 8 - k
            entry = inputs_ref[pl.ds(t, 1), :]
            slope = slope + entry * ramp
            adjoint = decay * adjoint + grad_ref[pl.ds(t, 1), :]
            total = total + entry * adjoint
            parts[pl.ds(pl.multiple_of(t * 8, 8), 8), :] = folded(read * adjoint)
            ramp = decay * ramp + adjoint
        return adjoint, ramp, total, slope

    _, ramp, total, slope = lax.fori_loop(
        0, rows // 8, lap, (adjoint_ref[...], zero, zero, zero)
    )
    sum_ref[...] = total
    slope_ref[...] = slope + enter_ref[...] * ramp
    grad = grad_ref[...]
    grad_inputs = unfold(parts, rows) + skip_ref[...] * grad
    grad_value_ref[...] = (grad_inputs * shifted_ref[...]).astype(BF16)
    grad_shifted = grad_inputs * value_ref[...]
    pad[0:rows, :] = grad_shifted
    pad[rows:, :] = jnp.zeros_like(head_ref)
    head_ref[...] = pad[0:8, :]
    grad_key = taps_ref[0:1, :] * grad_shifted
    for j in range(1, 4):
        grad_key = grad_key + taps_ref[j : j + 1, :] * pad[j : j + rows, :]
    grad_key_ref[...] = grad_key
    pad[0:8, :] = rim_ref[...]
    pad[8:, :] = key_ref[...]
    small = [
        jnp.sum(grad_shifted * pad[8 - j : 8 - j + rows, :], 0, keepdims=True) for j in range(4)
    ]
    small.append(jnp.sum(grad * inputs_ref[...], 0, keepdims=True))
    small.append(jnp.zeros((3, LANES), F32))
    small_ref[...] = jnp.concatenate(small, 0)


def bits_of(count):
    out, step = [], 1
    while step < count:
        out.append(step)
        step *= 2
    return out


class Wires:
    def __init__(self):
        self.batch, self.seq = lax.axis_size("batch"), lax.axis_size("seq")
        bits = bits_of(self.seq)
        swapped = bits[1::-1] + bits[2:]
        self.orders = (tuple(bits), tuple(swapped))
        self.stages = [(k,) for k in range(len(bits))]
        self.spare = bits_of(self.batch)[1:]
        self.core = lax.axis_index("batch") % 2
        self.place = lax.axis_index("seq")

    def spot(self, stage, core=None):
        core = self.core if core is None else core
        numbers = []
        for order in self.orders:
            digits = [(self.place // order[k]) % 2 for k in self.stages[stage]]
            numbers.append(sum(d * 2**i for i, d in enumerate(digits)))
        return jnp.where(core == 0, *numbers)

    def swap(self, value, stage, flip=1):
        pairs = []
        for b in range(self.batch):
            order = self.orders[b % 2]
            step = sum(order[k] for i, k in enumerate(self.stages[stage]) if flip // 2**i % 2)
            pairs += [(b * self.seq + s, b * self.seq + (s ^ step)) for s in range(self.seq)]
        return lax.ppermute(value, ("batch", "seq"), pairs)

    def swap_batch(self, value, step):
        return lax.ppermute(value, "batch", [(b, b ^ step) for b in range(self.batch)])

    def other_core(self, value):
        return self.swap_batch(value.astype(F32), 1)

    def joined(self, pieces, shape, kind, tail=0):
        rows, width = pieces[0].shape
        main = rows - tail
        here, there = self.spot(0), self.spot(0, 1 - self.core)
        places = jnp.stack([self.core, here, here ^ 1, there, there ^ 1]).astype(jnp.int32)
        outs = [jax.ShapeDtypeStruct(shape, F32)] * (2 if kind == "tensors" else 1)
        if tail:
            outs = outs + [jax.ShapeDtypeStruct((4 * tail, width), F32)]

        def kernel(places_ref, *refs):
            sources, targets, (buffer, sems_in, sems_out) = refs[:4], refs[4:-3], refs[-3:]
            reads = [
                pltpu.make_async_copy(sources[k], buffer.at[k], sems_in.at[k]) for k in range(4)
            ]
            for read in reads:
                read.start()
            core = places_ref[0]
            for k in range(4):
                reads[k].wait()
                owner = core if k < 2 else 1 - core
                spot = places_ref[1 + k]
                block = buffer.at[k, pl.ds(0, main)]

                def send(target, k=k, block=block):
                    pltpu.make_async_copy(block, target, sems_out.at[k]).start()

                if kind == "tensors":
                    for which in range(2):
                        window = targets[which].at[pl.ds(pl.multiple_of(spot * main, 8), main)]
                        pl.when(owner == which)(lambda window=window, send=send: send(window))
                elif kind == "rows":
                    place = pl.multiple_of((2 * owner + spot) * main, 8)
                    send(targets[0].at[pl.ds(place, main)])
                else:
                    place = pl.multiple_of(spot * main, 8)
                    column = pl.multiple_of(owner * width, LANES)
                    send(targets[0].at[pl.ds(place, main), pl.ds(column, width)])
                if tail:
                    place = pl.multiple_of((2 * owner + spot) * tail, 8)
                    pltpu.make_async_copy(
                        buffer.at[k, pl.ds(main, tail)],
                        targets[-1].at[pl.ds(place, tail)],
                        sems_out.at[4 + k],
                    ).start()
            for k in range(4):
                window = targets[0].at[pl.ds(0, main), pl.ds(0, width)]
                pltpu.make_async_copy(buffer.at[k, pl.ds(0, main)], window, sems_out.at[k]).wait()
                if tail:
                    pltpu.make_async_copy(
                        buffer.at[k, pl.ds(main, tail)],
                        targets[-1].at[pl.ds(0, tail)],
                        sems_out.at[4 + k],
                    ).wait()

        moved = 4 * rows * width * 4
        return pl.pallas_call(
            kernel,
            in_specs=[pl.BlockSpec(memory_space=pltpu.SMEM)]
            + [pl.BlockSpec(memory_space=pl.ANY)] * 4,
            out_specs=[pl.BlockSpec(memory_space=pl.ANY)] * len(outs),
            out_shape=outs,
            scratch_shapes=[
                pltpu.VMEM((4, rows, width), F32),
                pltpu.SemaphoreType.DMA((4,)),
                pltpu.SemaphoreType.DMA((8,)),
            ],
            cost_estimate=cost(2 * moved / 3.4e6),
            compiler_params=pltpu.CompilerParams(vmem_limit_bytes=moved + 4 * 1024 * 1024),
        )(places, *pieces)


def part(value, which, count, axis=0):
    size = value.shape[axis] // count
    return lax.dynamic_slice_in_dim(value, which * size, size, axis)


class Turns:
    def __init__(self, strict):
        self.strict, self.made = strict, None

    def take(self, value):
        if not self.strict or self.made is None:
            return value
        return lax.optimization_barrier((value, self.made))[0]

    def give(self, made):
        self.made = made


class Sum:
    def __init__(self, wires, turns, left, right, tail=None):
        self.wires, self.turns = wires, turns
        self.left, self.right, self.tail = left, right, tail
        self.count = len(wires.stages)

    def step(self, number):
        if number == 0:
            self.begin()
        elif number < self.count:
            self.scatter(number)
        else:
            self.gather(2 * self.count - 1 - number)

    def begin(self):
        wires, turns = self.wires, self.turns
        spot = wires.spot(0)
        left = turns.take(self.left)

        def piece(which):
            made = weight_grad(part(left, which, 2, 1), self.right)
            if self.tail is not None:
                made = jnp.concatenate([made, sum(part(x, which, 2) for x in self.tail)], 0)
            return made

        send = piece(1 - spot)
        arriving = wires.swap(send, 0)
        keep = piece(spot)
        turns.give((send, keep))
        self.terms = [keep, arriving]

    def scatter(self, stage):
        wires, turns = self.wires, self.turns
        ways = 2 ** len(wires.stages[stage])
        spot = wires.spot(stage)
        terms = self.terms[:-1] + [turns.take(self.terms[-1])]
        sends = [sum(part(t, spot ^ flip, ways) for t in terms) for flip in range(1, ways)]
        turns.give(sends)
        arriving = [wires.swap(send, stage, flip + 1) for flip, send in enumerate(sends)]
        self.terms = [sum(part(t, spot, ways) for t in terms)] + arriving

    def gather(self, stage):
        wires, turns = self.wires, self.turns
        if stage == self.count - 1:
            block = sum(self.terms[:-1]) + turns.take(self.terms[-1])
            for step in wires.spare:
                block = block + wires.swap_batch(block, step)
        else:
            ways = 2 ** len(wires.stages[stage + 1])
            spot = wires.spot(stage + 1)
            pieces = self.pieces[:-1] + [turns.take(self.pieces[-1])]
            rows = []
            for where in range(ways):
                picked = pieces[0]
                for flip in range(1, ways):
                    picked = jnp.where(spot == where ^ flip, pieces[flip], picked)
                rows.append(picked)
            block = jnp.concatenate(rows, 0)
        turns.give(block)
        ways = 2 ** len(wires.stages[stage])
        self.pieces = [block] + [wires.swap(block, stage, flip) for flip in range(1, ways)]
        if stage == 0:
            self.far = wires.swap_batch(block, 1)

    def cross(self):
        self.pieces[1] = self.turns.take(self.pieces[1])
        self.turns.give(self.pieces[1])
        self.far_other = self.wires.swap_batch(self.pieces[1], 1)

    def join(self, shape, kind, tail=0):
        pieces = (*self.pieces, self.far, self.turns.take(self.far_other))
        whole = self.wires.joined(pieces, shape, kind, tail)
        self.turns.give(whole[0])
        return whole


ORDER = (
    "X", "A00", "G1", "G2", "K1", "P", "A10", "P", "A01", "P",
    "A02", "A20", "B0", "A12", "A30", "A11", "A22", "R", "A40", "E",
    "A21", "A03", "A50", "A32", "A42", "A13", "A31", "A52", "A60", "A23",
    "A41", "A62", "A70", "A33", "A51", "A61", "F0", "A43", "A72", "A53",
    "A71", "F2", "J0", "A63", "A73", "F1", "J2", "J1", "F3", "J3",
)


def plain_order(sums, stages):
    names = ["X", "G1", "G2", "K1", "B0", "R", "E"]
    kinds = [f"A{k}" for k in range(2 * stages)] + ["F", "J"]
    return names + [f"{kind}{c}" for kind in kinds for c in range(sums)]


class Prefix:
    def __init__(self, turns, ends, rate, rows, backward):
        self.turns, self.rate, self.rows = turns, rate, rows
        self.count = lax.axis_size("seq")
        place = lax.axis_index("seq")
        self.rank = self.count - 1 - place if backward else place
        self.bits = bits_of(self.count)
        self.total, self.entering = ends, jnp.zeros_like(ends)
        self.done = 0
        self.start()

    def start(self):
        step = self.bits[self.done]
        pairs = [(s, s ^ step) for s in range(self.count)]
        self.arriving = lax.ppermute(self.total, "seq", pairs)

    def step(self):
        step = self.bits[self.done]
        arriving = self.turns.take(self.arriving)
        upper = (self.rank // step) % 2 == 1
        behind = ((self.rank % step) * self.rows).astype(F32)
        decayed = jnp.exp(-self.rate * behind) * arriving
        self.entering = jnp.where(upper, self.entering + decayed, self.entering)
        self.done += 1
        if self.done < len(self.bits):
            early = jnp.where(upper, arriving, self.total)
            late = jnp.where(upper, self.total, arriving)
            self.total = jnp.exp(-self.rate * (step * self.rows)) * early + late
            self.turns.give(self.total)
            self.start()

    def finish(self):
        while self.done < len(self.bits):
            self.step()
        return self.entering


def layer_norm(rows_in, gain):
    centred = rows_in - jnp.mean(rows_in, -1, keepdims=True)
    spread = jnp.mean(centred * centred, -1, keepdims=True)
    return centred * lax.rsqrt(spread + 1e-05) * gain


def gelu_tanh(upper):
    return jax.nn.gelu(upper, approximate=True)


def product(left, right):
    return jnp.dot(left, right, preferred_element_type=F32)


def weight_grad(left, right):
    return jnp.einsum("ti,tj->ij", left, right, preferred_element_type=F32)


def back_product(grad_rows, weight):
    return jnp.einsum("tj,ij->ti", grad_rows, weight, preferred_element_type=F32)


def local(
    tokens,
    w_query,
    w_key,
    w_value,
    w_out,
    w_up,
    w_down,
    gain_mix,
    gain_ffn,
    taps,
    rate,
    gain_b,
    gain_c,
    skip,
    cotangent,
):
    _, rows, width = tokens.shape
    count = lax.axis_size("seq")
    states = rate.shape[0]
    wires = Wires()
    skip_row = skip.reshape(1, width)
    scale = gain_b * jnp.sqrt(-jnp.expm1(-2.0 * rate))
    read = gain_c * scale

    flat_in = tokens.astype(F32).reshape(rows, width)
    normed, norm_pull = jax.vjp(layer_norm, flat_in, gain_mix)
    mixed_in = normed.astype(BF16)
    grad_out = cotangent.reshape(rows, width)
    all_grad_out = both(grad_out, wires.other_core(grad_out))
    all_mixed_in = both(mixed_in, wires.other_core(mixed_in))
    rim_own = product(layer_norm(flat_in[rows - 8 :], gain_mix).astype(BF16), w_key)
    rim = lax.ppermute(rim_own, "seq", [(s, s + 1) for s in range(count - 1)])
    queries = product(mixed_in, w_query)
    key_rows = product(mixed_in, w_key)
    values = product(mixed_in, w_value)
    share = rows * states * width / (256 * 64 * 768)
    shifted, inputs, ends = per_group(
        ends_kernel,
        (key_rows, values, rim, taps, rate),
        ((rows, F32), (rows, F32), (states, F32)),
        [pltpu.VMEM((rows + 8, LANES), F32)],
        4.3 * share,
    )
    entering = Prefix(Turns(False), ends, rate, rows, False).finish()
    mixed, gated = per_group(
        mix_kernel,
        (inputs, queries, entering, rate, read, skip_row),
        ((rows, F32), (rows, BF16)),
        [pltpu.VMEM((rows * 8, LANES), F32)],
        8.2 * share,
    )
    hidden = flat_in + product(gated, w_out)
    ffn_normed, ffn_pull = jax.vjp(layer_norm, hidden, gain_ffn)
    ffn_in = ffn_normed.astype(BF16)
    upper = product(ffn_in, w_up)
    activated, gelu_pull = jax.vjp(gelu_tanh, upper)
    act = activated.astype(BF16)

    strict = len(wires.stages) == 4
    turns = Turns(strict)
    sums, made, whole = {}, {}, {}
    first = wires.core == 0

    def own(value, axis=1):
        return part(value, wires.core, 2, axis)

    def others(value, axis=1):
        return part(value, 1 - wires.core, 2, axis)

    def forward_over():
        all_act = both(own(act), wires.other_core(others(act)))
        sums[0] = Sum(wires, turns, all_act, all_grad_out)
        made["ffn_in"] = both(ffn_in, wires.other_core(ffn_in))

    def up_back():
        grad_act = back_product(turns.take(grad_out), w_down)
        grad_upper = gelu_pull(grad_act)[0].astype(BF16)
        made["grad_upper"] = grad_upper
        turns.give(grad_upper)
        right = both(own(grad_upper), wires.other_core(others(grad_upper)))
        sums[1] = Sum(wires, turns, made["ffn_in"], right)

    def branch_back():
        grad_ffn = back_product(turns.take(made["grad_upper"]), w_up)
        grad_hidden_norm, made["d_gain_ffn"] = ffn_pull(grad_ffn)
        made["grad_hidden"] = grad_out.astype(F32) + grad_hidden_norm
        made["grad_branch"] = made["grad_hidden"].astype(BF16)
        made["grad_gated"] = back_product(made["grad_branch"], w_out)
        turns.give(made["grad_gated"])

    def towards():
        made["grad_queries"], made["grad_mixed"], starts = per_group(
            towards_kernel,
            (turns.take(made["grad_gated"]), queries, mixed, rate),
            ((rows, BF16), (rows, F32), (states, F32)),
            [],
            4.8 * share,
        )
        turns.give(starts)
        all_gated = both(gated, wires.other_core(gated))
        sent = jnp.where(first, made["grad_queries"], made["grad_branch"])
        kept = jnp.where(first, made["grad_branch"], made["grad_queries"])
        left = jnp.where(first, all_gated, all_mixed_in)
        sums[2] = Sum(wires, turns, left, both(kept, wires.other_core(sent)))
        made["prefix"] = Prefix(turns, starts, rate, rows, True)

    def mixer_back():
        adjoint = turns.take(made["prefix"].finish())
        out = per_group(
            back_kernel,
            (
                made["grad_mixed"],
                inputs,
                shifted,
                values,
                key_rows,
                rim,
                taps,
                rate,
                read,
                skip_row,
                entering,
                adjoint,
            ),
            ((rows, BF16), (rows, F32), (8, F32), (states, F32), (states, F32), (8, F32)),
            [pltpu.VMEM((rows * 8, LANES), F32), pltpu.VMEM((rows + 8, LANES), F32)],
            23 * share,
        )
        made["grad_values"], made["grad_keys"], head, *made["small"] = out
        turns.give(head)
        made["behind"] = lax.ppermute(head, "seq", [(s + 1, s) for s in range(count - 1)])

    def rim_back():
        behind, local_keys = turns.take(made["behind"]), made["grad_keys"]
        padded = jnp.concatenate([jnp.zeros_like(behind), behind[:4]], 0)
        late = sum(taps[j] * padded[j : j + 8] for j in range(1, 4))
        made["grad_keys"] = jnp.concatenate(
            [local_keys[: rows - 8], local_keys[rows - 8 :] + late], 0
        ).astype(BF16)
        turns.give(made["grad_keys"])
        sent = jnp.where(first, made["grad_values"], made["grad_keys"])
        kept = jnp.where(first, made["grad_keys"], made["grad_values"])
        made["both"] = both(kept, wires.other_core(sent))

    def input_back():
        grad_normed = (
            back_product(turns.take(made["grad_keys"]), w_key)
            + back_product(made["grad_queries"], w_query)
            + back_product(made["grad_values"], w_value)
        )
        grad_input_norm, made["d_gain_mix"] = norm_pull(grad_normed)
        made["d_tokens"] = (made["grad_hidden"] + grad_input_norm).astype(BF16)
        turns.give(made["d_tokens"])

        totals, slopes, small = made["small"]
        gains = jnp.stack([made["d_gain_mix"], made["d_gain_ffn"]])
        part_a = jnp.concatenate([totals, small[:5], jnp.zeros((extra - states - 5, width), F32)], 0)
        part_b = jnp.concatenate([slopes, gains, jnp.zeros((extra - states - 2, width), F32)], 0)
        tail = (
            jnp.where(first, part_a, part_b),
            wires.swap_batch(jnp.where(first, part_b, part_a), 1),
        )
        sums[3] = Sum(wires, turns, all_mixed_in, made["both"], tail)

    extra = 2 * 64 * (-(-(states + 5) // 128))
    joins = (
        (w_down.shape, "rows"),
        (w_up.shape, "columns"),
        (w_out.shape, "tensors"),
        (w_key.shape, "tensors", extra // 2),
    )
    steps = {
        "X": forward_over,
        "G1": up_back,
        "G2": branch_back,
        "K1": towards,
        "P": lambda: made["prefix"].step(),
        "B0": mixer_back,
        "R": rim_back,
        "E": input_back,
    }
    for name in ORDER if strict and ORDER else plain_order(4, len(wires.stages)):
        with jax.named_scope(name):
            if name[0] == "A":
                sums[int(name[-1])].step(int(name[1:-1]))
            elif name[0] == "F":
                sums[int(name[-1])].cross()
            elif name[0] == "J":
                whole[int(name[-1])] = sums[int(name[-1])].join(*joins[int(name[-1])])
            else:
                steps[name]()
    output = hidden + product(act, w_down)
    d_down, d_up = whole[0][0], whole[1][0]
    d_out, d_query = whole[2]
    d_key, d_value, tails = whole[3]
    part_a, part_b = tails[:extra], tails[extra:]
    d_tokens = made["d_tokens"].reshape(tokens.shape)
    totals, slopes = part_a[:states], part_b[:states]
    d_scale = gain_c * totals
    d_decay = read * slopes
    root = jnp.sqrt(-jnp.expm1(-2.0 * rate))
    d_rate = -jnp.exp(-rate) * d_decay + d_scale * gain_b * jnp.exp(-2.0 * rate) / root
    return (
        output.astype(BF16).reshape(tokens.shape),
        d_tokens,
        d_query,
        d_key,
        d_value,
        d_out,
        d_up,
        d_down,
        part_b[states],
        part_b[states + 1],
        part_a[states : states + 4],
        d_rate,
        d_scale * root,
        scale * totals,
        part_a[states + 4],
    )


def half_columns(value, which):
    columns = value.shape[1] // 2
    return lax.dynamic_slice_in_dim(value, which * columns, columns, 1)


def solution(mesh):
    split = P("batch", "seq", None)
    in_specs = (split,) + (P(),) * 13 + (split,)
    out_specs = (split, split) + (P(),) * 13
    return jax.shard_map(local, mesh=mesh, in_specs=in_specs, out_specs=out_specs, check_vma=False)
```

```python
import jax
import jax.numpy as jnp
from jax import lax
from jax.experimental import pallas as pl
from jax.experimental.pallas import tpu as pltpu
from jax.sharding import PartitionSpec as P

F32 = jnp.float32
BF16 = jnp.bfloat16
LANES = 128


def cost(micros):
    return pl.CostEstimate(flops=0, bytes_accessed=int(micros * 3.4e6), transcendentals=0)


def per_group(kernel, ins, outs, scratch, micros, groups=None, into=None):
    width = ins[0].shape[1]
    low, high = groups or (0, width // LANES)
    held = list(into or [])

    def spec(rows):
        return pl.BlockSpec((rows, LANES), lambda g: (0, g + low))

    def body(*refs):
        kernel(*refs[: len(ins)], *refs[len(ins) + len(held) :])

    return pl.pallas_call(
        body,
        grid=(high - low,),
        in_specs=[spec(x.shape[0]) for x in ins] + [pl.BlockSpec(memory_space=pl.ANY)] * len(held),
        out_specs=[spec(rows) for rows, _ in outs],
        out_shape=[jax.ShapeDtypeStruct((rows, width), kind) for rows, kind in outs],
        input_output_aliases={len(ins) + i: i for i in range(len(held))},
        scratch_shapes=scratch,
        cost_estimate=cost(micros * (high - low) * LANES / width),
        compiler_params=pltpu.CompilerParams(vmem_limit_bytes=32 * 1024 * 1024),
    )(*ins, *held)


def thirds(width):
    count = width // LANES
    cuts = [0, count // 3, 2 * count // 3, count]
    return [(low, high) for low, high in zip(cuts, cuts[1:]) if high > low]


def folded(product):
    return jnp.sum(product.reshape(product.shape[0] // 8, 8, product.shape[1]), 0)


def unfold(parts_ref, rows):
    total = parts_ref[pl.ds(0, rows, stride=8), :]
    for s in range(1, 8):
        total = total + parts_ref[pl.ds(s, rows, stride=8), :]
    return total


def both_kernel(own_ref, far_ref, out_ref):
    rows = own_ref.shape[0]
    out_ref[0:rows, :] = own_ref[...]
    out_ref[rows:, :] = far_ref[...].astype(BF16)


def both(own, far):
    rows, width = own.shape
    block = 3 * LANES
    return pl.pallas_call(
        both_kernel,
        grid=(width // block,),
        in_specs=[pl.BlockSpec((rows, block), lambda g: (0, g))] * 2,
        out_specs=pl.BlockSpec((2 * rows, block), lambda g: (0, g)),
        out_shape=jax.ShapeDtypeStruct((2 * rows, width), BF16),
        cost_estimate=cost(rows * width * 10 / 3.4e6),
    )(own, far)


def ends_kernel(key_ref, value_ref, rim_ref, taps_ref, rate_ref, shifted_ref, inputs_ref, end_ref, pad):
    rows = key_ref.shape[0]
    pad[0:8, :] = rim_ref[...]
    pad[8:, :] = key_ref[...]
    shifted = taps_ref[0:1, :] * pad[8:, :]
    for j in range(1, 4):
        shifted = shifted + taps_ref[j : j + 1, :] * pad[8 - j : 8 - j + rows, :]
    shifted_ref[...] = shifted
    inputs_ref[...] = shifted * value_ref[...]
    decay = jnp.exp(-rate_ref[...])

    def lap(i, state):
        for k in range(16):
            state = decay * state + inputs_ref[pl.ds(i * 16 + k, 1), :]
        return state

    end_ref[...] = lax.fori_loop(0, rows // 16, lap, jnp.zeros_like(decay))


def mix_kernel(inputs_ref, rate_ref, read_ref, skip_ref, mixed_ref, ramp_ref, parts):
    rows = inputs_ref.shape[0]
    decay = jnp.exp(-rate_ref[...])
    read = read_ref[...]
    zero = jnp.zeros_like(decay)

    def lap(i, carry):
        state, ramp = carry
        for k in range(8):
            t = i * 8 + k
            ramp = decay * (ramp + state)
            state = decay * state + inputs_ref[pl.ds(t, 1), :]
            parts[pl.ds(pl.multiple_of(t * 8, 8), 8), :] = folded(read * state)
        return state, ramp

    _, ramp_ref[...] = lax.fori_loop(0, rows // 8, lap, (zero, zero))
    mixed_ref[...] = unfold(parts, rows) + skip_ref[...] * inputs_ref[...]


def enter_kernel(
    local_ref, query_ref, enter_ref, rate_ref, read_ref, mixed_ref, gated_ref, parts
):
    rows = local_ref.shape[0]
    decay = jnp.exp(-rate_ref[...])

    def lap(i, state):
        for k in range(16):
            t = i * 16 + k
            state = decay * state
            parts[pl.ds(pl.multiple_of(t * 8, 8), 8), :] = folded(state)
        return state

    lax.fori_loop(0, rows // 16, lap, read_ref[...] * enter_ref[...])
    mixed = local_ref[...] + unfold(parts, rows)
    mixed_ref[...] = mixed
    gated_ref[...] = (query_ref[...] * mixed).astype(BF16)


def towards_kernel(
    grad_ref, query_ref, mixed_ref, rate_ref, grad_query_ref, grad_mixed_ref, start_ref
):
    rows = grad_ref.shape[0]
    grad_query_ref[...] = (grad_ref[...] * mixed_ref[...]).astype(BF16)
    grad_mixed_ref[...] = grad_ref[...] * query_ref[...]
    decay = jnp.exp(-rate_ref[...])

    def lap(i, state):
        for k in range(16):
            state = decay * state + grad_mixed_ref[pl.ds(rows - 1 - i * 16 - k, 1), :]
        return state

    start_ref[...] = lax.fori_loop(0, rows // 16, lap, jnp.zeros_like(decay))


def back_kernel(
    grad_ref, inputs_ref, rate_ref, read_ref, skip_ref, out_ref, sum_ref, slope_ref, ramp_ref, parts
):
    rows = grad_ref.shape[0]
    decay = jnp.exp(-rate_ref[...])
    read = read_ref[...]
    zero = jnp.zeros_like(decay)

    def lap(i, carry):
        adjoint, ramp, total, slope = carry
        for k in range(8):
            t = rows - 1 - i * 8 - k
            entry = inputs_ref[pl.ds(t, 1), :]
            slope = slope + entry * ramp
            adjoint = decay * adjoint + grad_ref[pl.ds(t, 1), :]
            total = total + entry * adjoint
            parts[pl.ds(pl.multiple_of(t * 8, 8), 8), :] = folded(read * adjoint)
            ramp = decay * ramp + adjoint
        return adjoint, ramp, total, slope

    _, ramp_ref[...], sum_ref[...], slope_ref[...] = lax.fori_loop(
        0, rows // 8, lap, (zero, zero, zero, zero)
    )
    out_ref[...] = unfold(parts, rows) + skip_ref[...] * grad_ref[...]


def adjoint_kernel(
    local_ref,
    grad_ref,
    inputs_ref,
    shifted_ref,
    value_ref,
    key_ref,
    rim_ref,
    taps_ref,
    rate_ref,
    read_ref,
    enter_ref,
    adjoint_ref,
    end_ref,
    end_ramp_ref,
    own_sum_ref,
    own_slope_ref,
    ramp_ref,
    grad_value_ref,
    grad_key_ref,
    head_ref,
    sum_ref,
    slope_ref,
    small_ref,
    parts,
    pad,
):
    rows = grad_ref.shape[0]
    decay = jnp.exp(-rate_ref[...])
    adjoint, enter = adjoint_ref[...], enter_ref[...]

    def lap(i, state):
        for k in range(16):
            t = rows - 1 - i * 16 - k
            state = decay * state
            parts[pl.ds(pl.multiple_of(t * 8, 8), 8), :] = folded(state)
        return state

    lax.fori_loop(0, rows // 16, lap, read_ref[...] * adjoint)
    sum_ref[...] = own_sum_ref[...] + adjoint * decay * end_ref[...]
    whole = rows * jnp.exp(-rate_ref[...] * rows)
    slope_ref[...] = (
        own_slope_ref[...]
        + enter * ramp_ref[...]
        + adjoint * (end_ramp_ref[...] + whole * enter)
    )
    grad_inputs = local_ref[...] + unfold(parts, rows)
    grad_value_ref[...] = (grad_inputs * shifted_ref[...]).astype(BF16)
    grad_shifted = grad_inputs * value_ref[...]
    pad[0:rows, :] = grad_shifted
    pad[rows:, :] = jnp.zeros_like(head_ref)
    head_ref[...] = pad[0:8, :]
    grad_key = taps_ref[0:1, :] * grad_shifted
    for j in range(1, 4):
        grad_key = grad_key + taps_ref[j : j + 1, :] * pad[j : j + rows, :]
    grad_key_ref[...] = grad_key
    pad[0:8, :] = rim_ref[...]
    pad[8:, :] = key_ref[...]
    small = [
        jnp.sum(grad_shifted * pad[8 - j : 8 - j + rows, :], 0, keepdims=True) for j in range(4)
    ]
    small.append(jnp.sum(grad_ref[...] * inputs_ref[...], 0, keepdims=True))
    small.append(jnp.zeros((3, LANES), F32))
    small_ref[...] = jnp.zeros_like(small_ref)
    small_ref[0:8, :] = jnp.concatenate(small, 0)


def bits_of(count):
    out, step = [], 1
    while step < count:
        out.append(step)
        step *= 2
    return out


class Wires:
    def __init__(self, far_first=False):
        self.batch, self.seq = lax.axis_size("batch"), lax.axis_size("seq")
        bits = bits_of(self.seq)
        near, swapped, far = bits[:2], bits[1::-1], bits[2:]
        lead = far[:1] if far_first else []
        far = far[len(lead) :]
        self.orders = (tuple(lead + near + far), tuple(lead + swapped + far))
        self.stages = [(k,) for k in range(len(bits))]
        self.spare = bits_of(self.batch)[1:]
        self.core = lax.axis_index("batch") % 2
        self.place = lax.axis_index("seq")

    def spot(self, stage, core=None):
        core = self.core if core is None else core
        numbers = []
        for order in self.orders:
            digits = [(self.place // order[k]) % 2 for k in self.stages[stage]]
            numbers.append(sum(d * 2**i for i, d in enumerate(digits)))
        return jnp.where(core == 0, *numbers)

    def swap(self, value, stage, flip=1):
        pairs = []
        for b in range(self.batch):
            order = self.orders[b % 2]
            step = sum(order[k] for i, k in enumerate(self.stages[stage]) if flip // 2**i % 2)
            pairs += [(b * self.seq + s, b * self.seq + (s ^ step)) for s in range(self.seq)]
        return lax.ppermute(value, ("batch", "seq"), pairs)

    def swap_batch(self, value, step):
        return lax.ppermute(value, "batch", [(b, b ^ step) for b in range(self.batch)])

    def other_core(self, value):
        return self.swap_batch(value.astype(F32), 1)

    def joined(self, pieces, shape, kind, tail=0, column=0, into=None):
        rows, width = pieces[0].shape
        main = rows - tail
        here, there = self.spot(0), self.spot(0, 1 - self.core)
        places = jnp.stack([self.core, here, here ^ 1, there, there ^ 1]).astype(jnp.int32)
        outs = [jax.ShapeDtypeStruct(shape, F32)] * (2 if kind == "tensors" else 1)
        if tail:
            outs = outs + [jax.ShapeDtypeStruct((4 * tail, width), F32)]
        held = [] if into is None else [into]
        cuts = 4 if main % 32 == 0 else 1
        step = main // cuts

        def kernel(places_ref, *refs):
            sources, targets = refs[:4], refs[4 + len(held) : -3]
            buffer, sems_in, sems_out = refs[-3:]
            spans = [(i * step, step) for i in range(cuts)] + ([(main, tail)] if tail else [])
            reads = {}
            for i, (start, size) in enumerate(spans):
                for k in range(4):
                    window = pl.ds(start, size)
                    reads[k, i] = pltpu.make_async_copy(
                        sources[k].at[window], buffer.at[k, window], sems_in.at[k, i]
                    )
                    reads[k, i].start()
            core = places_ref[0]
            for i, (start, size) in enumerate(spans):
                for k in range(4):
                    reads[k, i].wait()
                    owner = core if k < 2 else 1 - core
                    spot = places_ref[1 + k]
                    block = buffer.at[k, pl.ds(start, size)]

                    def send(target, k=k, i=i, block=block):
                        pltpu.make_async_copy(block, target, sems_out.at[k, i]).start()

                    if i >= cuts:
                        place = pl.multiple_of((2 * owner + spot) * tail, 8)
                        send(targets[-1].at[pl.ds(place, tail)])
                    elif kind == "tensors":
                        window = pl.ds(pl.multiple_of(spot * main + start, 8), size)
                        for which in range(2):
                            target = targets[which].at[window]
                            pl.when(owner == which)(lambda target=target, send=send: send(target))
                    elif kind == "rows":
                        place = pl.multiple_of((2 * owner + spot) * main + start, 8)
                        send(targets[0].at[pl.ds(place, size), pl.ds(column, width)])
                    else:
                        place = pl.multiple_of(spot * main + start, 8)
                        aside = pl.multiple_of(owner * (shape[1] // 2) + column, LANES)
                        send(targets[0].at[pl.ds(place, size), pl.ds(aside, width)])
            for i, (start, size) in enumerate(spans):
                for k in range(4):
                    target = targets[-1] if i >= cuts else targets[0]
                    pltpu.make_async_copy(
                        buffer.at[k, pl.ds(start, size)],
                        target.at[pl.ds(0, size), pl.ds(0, width)],
                        sems_out.at[k, i],
                    ).wait()

        moved = 4 * rows * width * 4
        return pl.pallas_call(
            kernel,
            in_specs=[pl.BlockSpec(memory_space=pltpu.SMEM)]
            + [pl.BlockSpec(memory_space=pl.ANY)] * (4 + len(held)),
            out_specs=[pl.BlockSpec(memory_space=pl.ANY)] * len(outs),
            out_shape=outs,
            input_output_aliases={5: 0} if held else {},
            scratch_shapes=[
                pltpu.VMEM((4, rows, width), F32),
                pltpu.SemaphoreType.DMA((4, cuts + 1)),
                pltpu.SemaphoreType.DMA((4, cuts + 1)),
            ],
            cost_estimate=cost(2 * moved / 3.4e6),
            compiler_params=pltpu.CompilerParams(vmem_limit_bytes=moved + 4 * 1024 * 1024),
        )(places, *pieces, *held)


def part(value, which, count, axis=0):
    size = value.shape[axis] // count
    return lax.dynamic_slice_in_dim(value, which * size, size, axis)


class Turns:
    def __init__(self, strict):
        self.strict, self.made = strict, None

    def take(self, value):
        if not self.strict or self.made is None:
            return value
        return lax.optimization_barrier((value, self.made))[0]

    def give(self, made):
        self.made = made


class Sum:
    def __init__(self, wires, turns, left, right, tail=None):
        self.wires, self.turns = wires, turns
        self.left, self.right, self.tail = left, right, tail
        self.count = len(wires.stages)

    def step(self, number):
        if number == 0:
            self.begin()
        elif number < self.count:
            self.scatter(number)
        else:
            self.gather(2 * self.count - 1 - number)

    def begin(self):
        wires, turns = self.wires, self.turns
        spot = wires.spot(0)
        left = turns.take(self.left)

        def piece(which):
            made = weight_grad(part(left, which, 2, 1), self.right)
            if self.tail is not None:
                rest = sum(jnp.where(which == 0, upper, lower) for upper, lower in self.tail)
                made = jnp.concatenate([made, rest], 0)
            return made

        send = piece(1 - spot)
        arriving = wires.swap(send, 0)
        keep = piece(spot)
        turns.give((send, keep))
        self.terms = [keep, arriving]

    def scatter(self, stage):
        wires, turns = self.wires, self.turns
        ways = 2 ** len(wires.stages[stage])
        spot = wires.spot(stage)
        terms = self.terms[:-1] + [turns.take(self.terms[-1])]
        sends = [sum(part(t, spot ^ flip, ways) for t in terms) for flip in range(1, ways)]
        turns.give(sends)
        arriving = [wires.swap(send, stage, flip + 1) for flip, send in enumerate(sends)]
        self.terms = [sum(part(t, spot, ways) for t in terms)] + arriving

    def gather(self, stage):
        wires, turns = self.wires, self.turns
        if stage == self.count - 1:
            block = sum(self.terms[:-1]) + turns.take(self.terms[-1])
            for step in wires.spare:
                block = block + wires.swap_batch(block, step)
        else:
            ways = 2 ** len(wires.stages[stage + 1])
            spot = wires.spot(stage + 1)
            pieces = self.pieces[:-1] + [turns.take(self.pieces[-1])]
            rows = []
            for where in range(ways):
                picked = pieces[0]
                for flip in range(1, ways):
                    picked = jnp.where(spot == where ^ flip, pieces[flip], picked)
                rows.append(picked)
            block = jnp.concatenate(rows, 0)
        turns.give(block)
        ways = 2 ** len(wires.stages[stage])
        self.pieces = [block] + [wires.swap(block, stage, flip) for flip in range(1, ways)]
        if stage == 0:
            self.far = wires.swap_batch(block, 1)

    def cross(self):
        self.pieces[1] = self.turns.take(self.pieces[1])
        self.turns.give(self.pieces[1])
        self.far_other = self.wires.swap_batch(self.pieces[1], 1)

    def join(self, shape, kind, tail=0, column=0, into=None):
        pieces = (*self.pieces, self.far, self.turns.take(self.far_other))
        whole = self.wires.joined(pieces, shape, kind, tail, column, into)
        self.turns.give(whole[0])
        return whole


FAR_FIRST = (False, False, False, False, False, False)

ORDER = (
    "X", "G1", "A01", "G2", "K1", "A00", "A11", "L2", "A04", "P",
    "A21", "A10", "L1", "A02", "P", "A14", "A20", "A03", "P", "L0",
    "A31", "A24", "B0", "A41", "A34", "R", "A13", "E", "A30", "A12",
    "A51", "A23", "A05", "A44", "A33", "A22", "A40", "A61", "A54", "A15",
    "A43", "A71", "A50", "A64", "A25", "A60", "A35", "A74", "A53", "A45",
    "A70", "A32", "A63", "A55", "A65", "A42", "F4", "A73", "A52", "F1",
    "A75", "A62", "F0", "J1", "J0", "J4", "F3", "A72", "O", "F5",
    "J3", "J5", "F2", "J2",
)


def plain_order(sums, stages):
    names = ["X", "G1", "G2", "K1", "L0", "L1", "L2", "O", "B0", "R", "E"]
    kinds = [f"A{k}" for k in range(2 * stages)] + ["F", "J"]
    return names + [f"{kind}{c}" for kind in kinds for c in range(sums)]


class Prefix:
    def __init__(self, turns, ends, rate, rows, backward):
        self.turns, self.rate, self.rows = turns, rate, rows
        self.count = lax.axis_size("seq")
        place = lax.axis_index("seq")
        self.rank = self.count - 1 - place if backward else place
        self.bits = bits_of(self.count)
        self.total, self.arrived = ends, []
        self.done = 0
        self.start()

    def start(self):
        step = self.bits[self.done]
        pairs = [(s, s ^ step) for s in range(self.count)]
        self.arriving = lax.ppermute(self.total, "seq", pairs)

    def step(self):
        step = self.bits[self.done]
        arriving = self.turns.take(self.arriving)
        upper = (self.rank // step) % 2 == 1
        self.arrived.append(arriving)
        self.done += 1
        if self.done < len(self.bits):
            early = jnp.where(upper, arriving, self.total)
            late = jnp.where(upper, self.total, arriving)
            self.total = jnp.exp(-self.rate * (step * self.rows)) * early + late
            self.turns.give(self.total)
            self.start()

    def finish(self):
        while self.done < len(self.bits):
            self.step()
        arrived = lax.optimization_barrier(self.arrived)
        entering = jnp.zeros_like(self.total)
        for step, value in zip(self.bits, arrived):
            behind = ((self.rank % step) * self.rows).astype(F32)
            upper = (self.rank // step) % 2 == 1
            entering = entering + jnp.where(upper, jnp.exp(-self.rate * behind) * value, 0.0)
        return entering


def layer_norm(rows_in, gain):
    centred = rows_in - jnp.mean(rows_in, -1, keepdims=True)
    spread = jnp.mean(centred * centred, -1, keepdims=True)
    return centred * lax.rsqrt(spread + 1e-05) * gain


def gelu_tanh(upper):
    return jax.nn.gelu(upper, approximate=True)


def product(left, right):
    return jnp.dot(left, right, preferred_element_type=F32)


def weight_grad(left, right):
    return jnp.einsum("ti,tj->ij", left, right, preferred_element_type=F32)


def back_product(grad_rows, weight):
    return jnp.einsum("tj,ij->ti", grad_rows, weight, preferred_element_type=F32)


def local(
    tokens,
    w_query,
    w_key,
    w_value,
    w_out,
    w_up,
    w_down,
    gain_mix,
    gain_ffn,
    taps,
    rate,
    gain_b,
    gain_c,
    skip,
    cotangent,
):
    _, rows, width = tokens.shape
    count = lax.axis_size("seq")
    states = rate.shape[0]
    wires = Wires()
    links = [Wires(far_first) for far_first in FAR_FIRST]
    skip_row = skip.reshape(1, width)
    scale = gain_b * jnp.sqrt(-jnp.expm1(-2.0 * rate))
    read = gain_c * scale

    flat_in = tokens.astype(F32).reshape(rows, width)
    normed, norm_pull = jax.vjp(layer_norm, flat_in, gain_mix)
    mixed_in = normed.astype(BF16)
    grad_out = cotangent.reshape(rows, width)
    rim_own = product(layer_norm(flat_in[rows - 8 :], gain_mix).astype(BF16), w_key)
    rim = lax.ppermute(rim_own, "seq", [(s, s + 1) for s in range(count - 1)])
    queries = product(mixed_in, w_query)
    key_rows = product(mixed_in, w_key)
    values = product(mixed_in, w_value)
    share = rows * states * width / (256 * 64 * 768)
    shifted, inputs, ends = per_group(
        ends_kernel,
        (key_rows, values, rim, taps, rate),
        ((rows, F32), (rows, F32), (states, F32)),
        [pltpu.VMEM((rows + 8, LANES), F32)],
        4.3 * share,
    )
    strict = len(wires.stages) == 4
    turns = Turns(strict)
    forward = Prefix(turns, ends, rate, rows, False)
    local_made = None
    for groups in thirds(width):
        local_made = per_group(
            mix_kernel,
            (turns.take(inputs), rate, read, skip_row),
            ((rows, F32), (states, F32)),
            [pltpu.VMEM((rows * 8, LANES), F32)],
            11 * share,
            groups,
            local_made,
        )
        turns.give(local_made)
        if forward.done == 0:
            far_grad_out = wires.other_core(turns.take(grad_out))
            far_mixed_in = wires.other_core(turns.take(mixed_in))
        if forward.done < len(forward.bits) - 1:
            forward.step()
    local_mixed, end_ramp = local_made
    all_grad_out = both(turns.take(grad_out), far_grad_out)
    all_mixed_in = both(mixed_in, far_mixed_in)
    turns.give((all_grad_out, all_mixed_in))
    entering = forward.finish()
    mixed, gated = per_group(
        enter_kernel,
        (local_mixed, queries, entering, rate, read),
        ((rows, F32), (rows, BF16)),
        [pltpu.VMEM((rows * 8, LANES), F32)],
        4.5 * share,
    )
    hidden = flat_in + product(gated, w_out)
    ffn_normed, ffn_pull = jax.vjp(layer_norm, hidden, gain_ffn)
    ffn_in = ffn_normed.astype(BF16)
    upper = product(ffn_in, w_up)
    activated, gelu_pull = jax.vjp(gelu_tanh, upper)
    act = activated.astype(BF16)

    turns = Turns(strict)
    sums, made, whole = {}, {"own": None}, {}
    first = wires.core == 0

    def own(value, axis=1):
        return part(value, wires.core, 2, axis)

    def others(value, axis=1):
        return part(value, 1 - wires.core, 2, axis)

    def forward_over():
        sent = others(act)
        turns.give(sent)
        all_act = both(own(act), wires.other_core(sent))
        right = all_grad_out.shape[1] // 2
        sums[0] = Sum(links[0], turns, all_act, all_grad_out[:, :right])
        sums[1] = Sum(links[1], turns, all_act, all_grad_out[:, right:])
        made["ffn_in"] = both(ffn_in, wires.other_core(turns.take(ffn_in)))

    def put_out():
        made["output"] = (hidden + product(turns.take(act), w_down)).astype(BF16)
        turns.give(made["output"])

    def up_back():
        grad_act = back_product(turns.take(grad_out), w_down)
        grad_upper = gelu_pull(grad_act)[0].astype(BF16)
        made["grad_upper"] = grad_upper
        turns.give(grad_upper)
        right = both(own(grad_upper), wires.other_core(others(grad_upper)))
        middle = right.shape[1] // 2
        sums[2] = Sum(links[2], turns, made["ffn_in"], right[:, :middle])
        sums[3] = Sum(links[3], turns, made["ffn_in"], right[:, middle:])

    def branch_back():
        grad_ffn = back_product(turns.take(made["grad_upper"]), w_up)
        grad_hidden_norm, made["d_gain_ffn"] = ffn_pull(grad_ffn)
        made["grad_hidden"] = grad_out.astype(F32) + grad_hidden_norm
        made["grad_branch"] = made["grad_hidden"].astype(BF16)
        made["grad_gated"] = back_product(made["grad_branch"], w_out)
        turns.give(made["grad_gated"])

    def towards():
        made["grad_queries"], made["grad_mixed"], starts = per_group(
            towards_kernel,
            (turns.take(made["grad_gated"]), queries, mixed, rate),
            ((rows, BF16), (rows, F32), (states, F32)),
            [],
            4.8 * share,
        )
        turns.give(starts)
        all_gated = both(gated, wires.other_core(gated))
        sent = jnp.where(first, made["grad_queries"], made["grad_branch"])
        kept = jnp.where(first, made["grad_branch"], made["grad_queries"])
        left = jnp.where(first, all_gated, all_mixed_in)
        sums[4] = Sum(links[4], turns, left, both(kept, wires.other_core(sent)))
        made["prefix"] = Prefix(turns, starts, rate, rows, True)

    def own_back(groups):
        made["own"] = per_group(
            back_kernel,
            (turns.take(made["grad_mixed"]), inputs, rate, read, skip_row),
            ((rows, F32), (states, F32), (states, F32), (states, F32)),
            [pltpu.VMEM((rows * 8, LANES), F32)],
            22 * share,
            groups,
            made["own"],
        )
        turns.give(made["own"])

    def mixer_back():
        adjoint = turns.take(made["prefix"].finish())
        local_grad, *own_sums = made["own"]
        out = per_group(
            adjoint_kernel,
            (
                local_grad,
                made["grad_mixed"],
                inputs,
                shifted,
                values,
                key_rows,
                rim,
                taps,
                rate,
                read,
                entering,
                adjoint,
                ends,
                end_ramp,
                *own_sums,
            ),
            ((rows, BF16), (rows, F32), (8, F32), (states, F32), (states, F32), (states, F32)),
            [pltpu.VMEM((rows * 8, LANES), F32), pltpu.VMEM((rows + 8, LANES), F32)],
            7 * share,
        )
        made["grad_values"], made["grad_keys"], head, *made["small"] = out
        turns.give(head)
        made["behind"] = lax.ppermute(head, "seq", [(s + 1, s) for s in range(count - 1)])

    def rim_back():
        behind, local_keys = turns.take(made["behind"]), made["grad_keys"]
        padded = jnp.concatenate([jnp.zeros_like(behind), behind[:4]], 0)
        late = sum(taps[j] * padded[j : j + 8] for j in range(1, 4))
        made["grad_keys"] = jnp.concatenate(
            [local_keys[: rows - 8], local_keys[rows - 8 :] + late], 0
        ).astype(BF16)
        turns.give(made["grad_keys"])
        sent = jnp.where(first, made["grad_values"], made["grad_keys"])
        kept = jnp.where(first, made["grad_keys"], made["grad_values"])
        made["both"] = both(kept, wires.other_core(sent))

    def input_back():
        grad_normed = (
            back_product(turns.take(made["grad_keys"]), w_key)
            + back_product(made["grad_queries"], w_query)
            + back_product(made["grad_values"], w_value)
        )
        grad_input_norm, made["d_gain_mix"] = norm_pull(grad_normed)
        made["d_tokens"] = (made["grad_hidden"] + grad_input_norm).astype(BF16)
        turns.give(made["d_tokens"])

        totals, slopes, small = made["small"]
        gains = jnp.stack([made["d_gain_mix"], made["d_gain_ffn"]])
        gains = jnp.pad(gains, ((0, states - 2), (0, 0)))
        upper = wires.swap_batch(jnp.where(first, slopes, totals), 1)
        lower = wires.swap_batch(jnp.where(first, gains, small), 1)
        tail = (
            (jnp.where(first, totals, slopes), jnp.where(first, small, gains)),
            (upper, lower),
        )
        sums[5] = Sum(links[5], turns, all_mixed_in, made["both"], tail)

    joins = (
        (w_down.shape, "rows", 0, 0),
        (w_down.shape, "rows", 0, width // 2),
        (w_up.shape, "columns", 0, 0),
        (w_up.shape, "columns", 0, w_up.shape[1] // 4),
        (w_out.shape, "tensors"),
        (w_key.shape, "tensors", states),
    )
    steps = {
        "X": forward_over,
        "O": put_out,
        "G1": up_back,
        "G2": branch_back,
        "K1": towards,
        "P": lambda: made["prefix"].step(),
        "L0": lambda: own_back(thirds(width)[0]),
        "L1": lambda: own_back(thirds(width)[1]),
        "L2": lambda: own_back(thirds(width)[2]),
        "B0": mixer_back,
        "R": rim_back,
        "E": input_back,
    }
    for name in ORDER if strict and ORDER else plain_order(6, len(wires.stages)):
        with jax.named_scope(name):
            if name[0] == "A":
                sums[int(name[-1])].step(int(name[1:-1]))
            elif name[0] == "F":
                sums[int(name[-1])].cross()
            elif name[0] == "J":
                number = int(name[-1])
                into = None
                if number < 4 and number ^ 1 in whole:
                    into = whole[number ^ 1][0]
                whole[number] = sums[number].join(*joins[number], into=into)
            else:
                steps[name]()
    last = list(whole)
    d_down, d_up = (whole[max(pair, key=last.index)][0] for pair in ((0, 1), (2, 3)))
    d_out, d_query = whole[4]
    d_key, d_value, tails = whole[5]
    part_a, part_b = tails[: 2 * states], tails[2 * states :]
    d_tokens = made["d_tokens"].reshape(tokens.shape)
    totals, slopes = part_a[:states], part_b[:states]
    d_scale = gain_c * totals
    d_decay = read * slopes
    root = jnp.sqrt(-jnp.expm1(-2.0 * rate))
    d_rate = -jnp.exp(-rate) * d_decay + d_scale * gain_b * jnp.exp(-2.0 * rate) / root
    return (
        made["output"].reshape(tokens.shape),
        d_tokens,
        d_query,
        d_key,
        d_value,
        d_out,
        d_up,
        d_down,
        part_b[states],
        part_b[states + 1],
        part_a[states : states + 4],
        d_rate,
        d_scale * root,
        scale * totals,
        part_a[states + 4],
    )


def half_columns(value, which):
    columns = value.shape[1] // 2
    return lax.dynamic_slice_in_dim(value, which * columns, columns, 1)


def solution(mesh):
    split = P("batch", "seq", None)
    in_specs = (split,) + (P(),) * 13 + (split,)
    out_specs = (split, split) + (P(),) * 13
    return jax.shard_map(local, mesh=mesh, in_specs=in_specs, out_specs=out_specs, check_vma=False)
```

```python
import jax
import jax.numpy as jnp
from jax import lax
from jax.experimental import pallas as pl
from jax.experimental.pallas import tpu as pltpu
from jax.sharding import PartitionSpec as P

F32 = jnp.float32
BF16 = jnp.bfloat16
LANES = 128


def cost(micros):
    return pl.CostEstimate(flops=0, bytes_accessed=int(micros * 3.4e6), transcendentals=0)


def per_group(kernel, ins, outs, scratch, micros, groups=None, into=None):
    width = ins[0].shape[1]
    low, high = groups or (0, width // LANES)
    held = list(into or [])

    def spec(rows):
        return pl.BlockSpec((rows, LANES), lambda g: (0, g + low))

    def body(*refs):
        kernel(*refs[: len(ins)], *refs[len(ins) + len(held) :])

    return pl.pallas_call(
        body,
        grid=(high - low,),
        in_specs=[spec(x.shape[0]) for x in ins] + [pl.BlockSpec(memory_space=pl.ANY)] * len(held),
        out_specs=[spec(rows) for rows, _ in outs],
        out_shape=[jax.ShapeDtypeStruct((rows, width), kind) for rows, kind in outs],
        input_output_aliases={len(ins) + i: i for i in range(len(held))},
        scratch_shapes=scratch,
        cost_estimate=cost(micros * (high - low) * LANES / width),
        compiler_params=pltpu.CompilerParams(vmem_limit_bytes=32 * 1024 * 1024),
    )(*ins, *held)


def thirds(width):
    count = width // LANES
    cuts = [0, count // 3, 2 * count // 3, count]
    return [(low, high) for low, high in zip(cuts, cuts[1:]) if high > low]


def folded(product):
    return jnp.sum(product.reshape(product.shape[0] // 8, 8, product.shape[1]), 0)


def unfold(parts_ref, rows):
    total = parts_ref[pl.ds(0, rows, stride=8), :]
    for s in range(1, 8):
        total = total + parts_ref[pl.ds(s, rows, stride=8), :]
    return total


def both_kernel(own_ref, far_ref, out_ref):
    rows = own_ref.shape[0]
    out_ref[0:rows, :] = own_ref[...]
    out_ref[rows:, :] = far_ref[...].astype(BF16)


def both(own, far):
    rows, width = own.shape
    block = 3 * LANES
    return pl.pallas_call(
        both_kernel,
        grid=(width // block,),
        in_specs=[pl.BlockSpec((rows, block), lambda g: (0, g))] * 2,
        out_specs=pl.BlockSpec((2 * rows, block), lambda g: (0, g)),
        out_shape=jax.ShapeDtypeStruct((2 * rows, width), BF16),
        cost_estimate=cost(rows * width * 10 / 3.4e6),
    )(own, far)


def ends_kernel(key_ref, value_ref, rim_ref, taps_ref, rate_ref, shifted_ref, inputs_ref, end_ref, pad):
    rows = key_ref.shape[0]
    pad[0:8, :] = rim_ref[...]
    pad[8:, :] = key_ref[...]
    shifted = taps_ref[0:1, :] * pad[8:, :]
    for j in range(1, 4):
        shifted = shifted + taps_ref[j : j + 1, :] * pad[8 - j : 8 - j + rows, :]
    shifted_ref[...] = shifted
    inputs_ref[...] = shifted * value_ref[...]
    decay = jnp.exp(-rate_ref[...])

    def lap(i, state):
        for k in range(16):
            state = decay * state + inputs_ref[pl.ds(i * 16 + k, 1), :]
        return state

    end_ref[...] = lax.fori_loop(0, rows // 16, lap, jnp.zeros_like(decay))


def mix_kernel(inputs_ref, rate_ref, read_ref, skip_ref, mixed_ref, ramp_ref, parts):
    rows = inputs_ref.shape[0]
    decay = jnp.exp(-rate_ref[...])
    read = read_ref[...]
    zero = jnp.zeros_like(decay)

    def lap(i, carry):
        state, ramp = carry
        for k in range(8):
            t = i * 8 + k
            ramp = decay * (ramp + state)
            state = decay * state + inputs_ref[pl.ds(t, 1), :]
            parts[pl.ds(pl.multiple_of(t * 8, 8), 8), :] = folded(read * state)
        return state, ramp

    _, ramp_ref[...] = lax.fori_loop(0, rows // 8, lap, (zero, zero))
    mixed_ref[...] = unfold(parts, rows) + skip_ref[...] * inputs_ref[...]


def enter_kernel(
    local_ref, query_ref, enter_ref, rate_ref, read_ref, mixed_ref, gated_ref, parts
):
    rows = local_ref.shape[0]
    decay = jnp.exp(-rate_ref[...])

    def lap(i, state):
        for k in range(16):
            t = i * 16 + k
            state = decay * state
            parts[pl.ds(pl.multiple_of(t * 8, 8), 8), :] = folded(state)
        return state

    lax.fori_loop(0, rows // 16, lap, read_ref[...] * enter_ref[...])
    mixed = local_ref[...] + unfold(parts, rows)
    mixed_ref[...] = mixed
    gated_ref[...] = (query_ref[...] * mixed).astype(BF16)


def towards_kernel(
    grad_ref, query_ref, mixed_ref, rate_ref, grad_query_ref, grad_mixed_ref, start_ref
):
    rows = grad_ref.shape[0]
    grad_query_ref[...] = (grad_ref[...] * mixed_ref[...]).astype(BF16)
    grad_mixed_ref[...] = grad_ref[...] * query_ref[...]
    decay = jnp.exp(-rate_ref[...])

    def lap(i, state):
        for k in range(16):
            state = decay * state + grad_mixed_ref[pl.ds(rows - 1 - i * 16 - k, 1), :]
        return state

    start_ref[...] = lax.fori_loop(0, rows // 16, lap, jnp.zeros_like(decay))


def back_kernel(
    grad_ref, inputs_ref, rate_ref, read_ref, skip_ref, out_ref, sum_ref, slope_ref, ramp_ref, parts
):
    rows = grad_ref.shape[0]
    decay = jnp.exp(-rate_ref[...])
    read = read_ref[...]
    zero = jnp.zeros_like(decay)

    def lap(i, carry):
        adjoint, ramp, total, slope = carry
        for k in range(8):
            t = rows - 1 - i * 8 - k
            entry = inputs_ref[pl.ds(t, 1), :]
            slope = slope + entry * ramp
            adjoint = decay * adjoint + grad_ref[pl.ds(t, 1), :]
            total = total + entry * adjoint
            parts[pl.ds(pl.multiple_of(t * 8, 8), 8), :] = folded(read * adjoint)
            ramp = decay * ramp + adjoint
        return adjoint, ramp, total, slope

    _, ramp_ref[...], sum_ref[...], slope_ref[...] = lax.fori_loop(
        0, rows // 8, lap, (zero, zero, zero, zero)
    )
    out_ref[...] = unfold(parts, rows) + skip_ref[...] * grad_ref[...]


def adjoint_kernel(
    local_ref,
    grad_ref,
    inputs_ref,
    shifted_ref,
    value_ref,
    key_ref,
    rim_ref,
    taps_ref,
    rate_ref,
    read_ref,
    enter_ref,
    adjoint_ref,
    end_ref,
    end_ramp_ref,
    own_sum_ref,
    own_slope_ref,
    ramp_ref,
    grad_value_ref,
    grad_key_ref,
    head_ref,
    sum_ref,
    slope_ref,
    small_ref,
    parts,
    pad,
):
    rows = grad_ref.shape[0]
    decay = jnp.exp(-rate_ref[...])
    adjoint, enter = adjoint_ref[...], enter_ref[...]

    def lap(i, state):
        for k in range(16):
            t = rows - 1 - i * 16 - k
            state = decay * state
            parts[pl.ds(pl.multiple_of(t * 8, 8), 8), :] = folded(state)
        return state

    lax.fori_loop(0, rows // 16, lap, read_ref[...] * adjoint)
    sum_ref[...] = own_sum_ref[...] + adjoint * decay * end_ref[...]
    whole = rows * jnp.exp(-rate_ref[...] * rows)
    slope_ref[...] = (
        own_slope_ref[...]
        + enter * ramp_ref[...]
        + adjoint * (end_ramp_ref[...] + whole * enter)
    )
    grad_inputs = local_ref[...] + unfold(parts, rows)
    grad_value_ref[...] = (grad_inputs * shifted_ref[...]).astype(BF16)
    grad_shifted = grad_inputs * value_ref[...]
    pad[0:rows, :] = grad_shifted
    pad[rows:, :] = jnp.zeros_like(head_ref)
    head_ref[...] = pad[0:8, :]
    grad_key = taps_ref[0:1, :] * grad_shifted
    for j in range(1, 4):
        grad_key = grad_key + taps_ref[j : j + 1, :] * pad[j : j + rows, :]
    grad_key_ref[...] = grad_key
    pad[0:8, :] = rim_ref[...]
    pad[8:, :] = key_ref[...]
    small = [
        jnp.sum(grad_shifted * pad[8 - j : 8 - j + rows, :], 0, keepdims=True) for j in range(4)
    ]
    small.append(jnp.sum(grad_ref[...] * inputs_ref[...], 0, keepdims=True))
    small.append(jnp.zeros((3, LANES), F32))
    small_ref[...] = jnp.zeros_like(small_ref)
    small_ref[0:8, :] = jnp.concatenate(small, 0)


def bits_of(count):
    out, step = [], 1
    while step < count:
        out.append(step)
        step *= 2
    return out


class Wires:
    def __init__(self, far_first=False):
        self.batch, self.seq = lax.axis_size("batch"), lax.axis_size("seq")
        bits = bits_of(self.seq)
        near, swapped, far = bits[:2], bits[1::-1], bits[2:]
        lead = far[:1] if far_first else []
        far = far[len(lead) :]
        self.orders = (tuple(lead + near + far), tuple(lead + swapped + far))
        self.stages = [(k,) for k in range(len(bits))]
        self.spare = bits_of(self.batch)[1:]
        self.core = lax.axis_index("batch") % 2
        self.place = lax.axis_index("seq")

    def spot(self, stage, core=None):
        core = self.core if core is None else core
        numbers = []
        for order in self.orders:
            digits = [(self.place // order[k]) % 2 for k in self.stages[stage]]
            numbers.append(sum(d * 2**i for i, d in enumerate(digits)))
        return jnp.where(core == 0, *numbers)

    def swap(self, value, stage, flip=1):
        pairs = []
        for b in range(self.batch):
            order = self.orders[b % 2]
            step = sum(order[k] for i, k in enumerate(self.stages[stage]) if flip // 2**i % 2)
            pairs += [(b * self.seq + s, b * self.seq + (s ^ step)) for s in range(self.seq)]
        return lax.ppermute(value, ("batch", "seq"), pairs)

    def swap_batch(self, value, step):
        return lax.ppermute(value, "batch", [(b, b ^ step) for b in range(self.batch)])

    def other_core(self, value):
        return self.swap_batch(value.astype(F32), 1)

    def joined(self, pieces, shape, kind, tail=0, column=0, into=None):
        rows, width = pieces[0].shape
        main = rows - tail
        here, there = self.spot(0), self.spot(0, 1 - self.core)
        places = jnp.stack([self.core, here, here ^ 1, there, there ^ 1]).astype(jnp.int32)
        outs = [jax.ShapeDtypeStruct(shape, F32)] * (2 if kind == "tensors" else 1)
        if tail:
            outs = outs + [jax.ShapeDtypeStruct((4 * tail, width), F32)]
        held = [] if into is None else [into]
        cuts = 4 if main % 32 == 0 else 1
        step = main // cuts

        def kernel(places_ref, *refs):
            sources, targets = refs[:4], refs[4 + len(held) : -3]
            buffer, sems_in, sems_out = refs[-3:]
            spans = [(i * step, step) for i in range(cuts)] + ([(main, tail)] if tail else [])
            reads = {}
            for i, (start, size) in enumerate(spans):
                for k in range(4):
                    window = pl.ds(start, size)
                    reads[k, i] = pltpu.make_async_copy(
                        sources[k].at[window], buffer.at[k, window], sems_in.at[k, i]
                    )
                    reads[k, i].start()
            core = places_ref[0]
            for i, (start, size) in enumerate(spans):
                for k in range(4):
                    reads[k, i].wait()
                    owner = core if k < 2 else 1 - core
                    spot = places_ref[1 + k]
                    block = buffer.at[k, pl.ds(start, size)]

                    def send(target, k=k, i=i, block=block):
                        pltpu.make_async_copy(block, target, sems_out.at[k, i]).start()

                    if i >= cuts:
                        place = pl.multiple_of((2 * owner + spot) * tail, 8)
                        send(targets[-1].at[pl.ds(place, tail)])
                    elif kind == "tensors":
                        window = pl.ds(pl.multiple_of(spot * main + start, 8), size)
                        for which in range(2):
                            target = targets[which].at[window]
                            pl.when(owner == which)(lambda target=target, send=send: send(target))
                    elif kind == "rows":
                        place = pl.multiple_of((2 * owner + spot) * main + start, 8)
                        send(targets[0].at[pl.ds(place, size), pl.ds(column, width)])
                    else:
                        place = pl.multiple_of(spot * main + start, 8)
                        aside = pl.multiple_of(owner * (shape[1] // 2) + column, LANES)
                        send(targets[0].at[pl.ds(place, size), pl.ds(aside, width)])
            for i, (start, size) in enumerate(spans):
                for k in range(4):
                    target = targets[-1] if i >= cuts else targets[0]
                    pltpu.make_async_copy(
                        buffer.at[k, pl.ds(start, size)],
                        target.at[pl.ds(0, size), pl.ds(0, width)],
                        sems_out.at[k, i],
                    ).wait()

        moved = 4 * rows * width * 4
        return pl.pallas_call(
            kernel,
            in_specs=[pl.BlockSpec(memory_space=pltpu.SMEM)]
            + [pl.BlockSpec(memory_space=pl.ANY)] * (4 + len(held)),
            out_specs=[pl.BlockSpec(memory_space=pl.ANY)] * len(outs),
            out_shape=outs,
            input_output_aliases={5: 0} if held else {},
            scratch_shapes=[
                pltpu.VMEM((4, rows, width), F32),
                pltpu.SemaphoreType.DMA((4, cuts + 1)),
                pltpu.SemaphoreType.DMA((4, cuts + 1)),
            ],
            cost_estimate=cost(2 * moved / 3.4e6),
            compiler_params=pltpu.CompilerParams(vmem_limit_bytes=moved + 4 * 1024 * 1024),
        )(places, *pieces, *held)


def part(value, which, count, axis=0):
    size = value.shape[axis] // count
    return lax.dynamic_slice_in_dim(value, which * size, size, axis)


class Turns:
    def __init__(self, strict):
        self.strict, self.made = strict, None

    def take(self, value):
        if not self.strict or self.made is None:
            return value
        return lax.optimization_barrier((value, self.made))[0]

    def give(self, made):
        self.made = made


class Sum:
    def __init__(self, wires, turns, left, right, tail=None):
        self.wires, self.turns = wires, turns
        self.left, self.right, self.tail = left, right, tail
        self.count = len(wires.stages)

    def step(self, number):
        if number == 0:
            self.begin()
        elif number < self.count:
            self.scatter(number)
        else:
            self.gather(2 * self.count - 1 - number)

    def begin(self):
        wires, turns = self.wires, self.turns
        spot = wires.spot(0)
        left = turns.take(self.left)

        def piece(which):
            made = weight_grad(part(left, which, 2, 1), self.right)
            if self.tail is not None:
                rest = sum(jnp.where(which == 0, upper, lower) for upper, lower in self.tail)
                made = jnp.concatenate([made, rest], 0)
            return made

        send = piece(1 - spot)
        arriving = wires.swap(send, 0)
        keep = piece(spot)
        turns.give((send, keep))
        self.terms = [keep, arriving]

    def scatter(self, stage):
        wires, turns = self.wires, self.turns
        ways = 2 ** len(wires.stages[stage])
        spot = wires.spot(stage)
        terms = self.terms[:-1] + [turns.take(self.terms[-1])]
        sends = [sum(part(t, spot ^ flip, ways) for t in terms) for flip in range(1, ways)]
        turns.give(sends)
        arriving = [wires.swap(send, stage, flip + 1) for flip, send in enumerate(sends)]
        self.terms = [sum(part(t, spot, ways) for t in terms)] + arriving

    def gather(self, stage):
        wires, turns = self.wires, self.turns
        if stage == self.count - 1:
            block = sum(self.terms[:-1]) + turns.take(self.terms[-1])
            for step in wires.spare:
                block = block + wires.swap_batch(block, step)
        else:
            ways = 2 ** len(wires.stages[stage + 1])
            spot = wires.spot(stage + 1)
            pieces = self.pieces[:-1] + [turns.take(self.pieces[-1])]
            rows = []
            for where in range(ways):
                picked = pieces[0]
                for flip in range(1, ways):
                    picked = jnp.where(spot == where ^ flip, pieces[flip], picked)
                rows.append(picked)
            block = jnp.concatenate(rows, 0)
        turns.give(block)
        ways = 2 ** len(wires.stages[stage])
        self.pieces = [block] + [wires.swap(block, stage, flip) for flip in range(1, ways)]
        if stage == 0:
            self.far = wires.swap_batch(block, 1)

    def cross(self):
        self.pieces[1] = self.turns.take(self.pieces[1])
        self.turns.give(self.pieces[1])
        self.far_other = self.wires.swap_batch(self.pieces[1], 1)

    def join(self, shape, kind, tail=0, column=0, into=None):
        pieces = (*self.pieces, self.far, self.turns.take(self.far_other))
        whole = self.wires.joined(pieces, shape, kind, tail, column, into)
        self.turns.give(whole[0])
        return whole


FAR_FIRST = (False, False, False, False, False, False)

ORDER = (
    "X", "G1", "A01", "G2", "K1", "A00", "A11", "L2", "A04", "P",
    "A21", "A10", "L1", "A02", "P", "A14", "A20", "A03", "P", "L0",
    "A31", "A24", "B0", "A41", "A34", "R", "A13", "E", "A30", "A12",
    "A51", "A23", "A05", "A44", "A33", "A22", "A40", "A61", "A54", "A15",
    "A43", "A71", "A50", "A64", "A25", "A60", "A35", "A74", "A53", "A45",
    "F1", "A70", "A32", "A63", "J1", "A55", "F4", "A65", "J4", "A42",
    "F0", "A73", "A52", "J0", "A75", "A62", "O", "F3", "A72", "J3",
    "F5", "J5", "F2", "J2",
)


def plain_order(sums, stages):
    names = ["X", "G1", "G2", "K1", "L0", "L1", "L2", "O", "B0", "R", "E"]
    kinds = [f"A{k}" for k in range(2 * stages)] + ["F", "J"]
    return names + [f"{kind}{c}" for kind in kinds for c in range(sums)]


class Prefix:
    def __init__(self, turns, ends, rate, rows, backward):
        self.turns, self.rate, self.rows = turns, rate, rows
        self.count = lax.axis_size("seq")
        place = lax.axis_index("seq")
        self.rank = self.count - 1 - place if backward else place
        self.bits = bits_of(self.count)
        self.total, self.arrived = ends, []
        self.done = 0
        self.start()

    def start(self):
        step = self.bits[self.done]
        pairs = [(s, s ^ step) for s in range(self.count)]
        self.arriving = lax.ppermute(self.total, "seq", pairs)

    def step(self):
        step = self.bits[self.done]
        arriving = self.turns.take(self.arriving)
        upper = (self.rank // step) % 2 == 1
        self.arrived.append(arriving)
        self.done += 1
        if self.done < len(self.bits):
            early = jnp.where(upper, arriving, self.total)
            late = jnp.where(upper, self.total, arriving)
            self.total = jnp.exp(-self.rate * (step * self.rows)) * early + late
            self.turns.give(self.total)
            self.start()

    def finish(self):
        while self.done < len(self.bits):
            self.step()
        arrived = lax.optimization_barrier(self.arrived)
        entering = jnp.zeros_like(self.total)
        for step, value in zip(self.bits, arrived):
            behind = ((self.rank % step) * self.rows).astype(F32)
            upper = (self.rank // step) % 2 == 1
            entering = entering + jnp.where(upper, jnp.exp(-self.rate * behind) * value, 0.0)
        return entering


def layer_norm(rows_in, gain):
    centred = rows_in - jnp.mean(rows_in, -1, keepdims=True)
    spread = jnp.mean(centred * centred, -1, keepdims=True)
    return centred * lax.rsqrt(spread + 1e-05) * gain


def gelu_tanh(upper):
    return jax.nn.gelu(upper, approximate=True)


def product(left, right):
    return jnp.dot(left, right, preferred_element_type=F32)


def weight_grad(left, right):
    return jnp.einsum("ti,tj->ij", left, right, preferred_element_type=F32)


def back_product(grad_rows, weight):
    return jnp.einsum("tj,ij->ti", grad_rows, weight, preferred_element_type=F32)


def local(
    tokens,
    w_query,
    w_key,
    w_value,
    w_out,
    w_up,
    w_down,
    gain_mix,
    gain_ffn,
    taps,
    rate,
    gain_b,
    gain_c,
    skip,
    cotangent,
):
    _, rows, width = tokens.shape
    count = lax.axis_size("seq")
    states = rate.shape[0]
    wires = Wires()
    links = [Wires(far_first) for far_first in FAR_FIRST]
    skip_row = skip.reshape(1, width)
    scale = gain_b * jnp.sqrt(-jnp.expm1(-2.0 * rate))
    read = gain_c * scale

    flat_in = tokens.astype(F32).reshape(rows, width)
    normed, norm_pull = jax.vjp(layer_norm, flat_in, gain_mix)
    mixed_in = normed.astype(BF16)
    grad_out = cotangent.reshape(rows, width)
    rim_own = product(layer_norm(flat_in[rows - 8 :], gain_mix).astype(BF16), w_key)
    rim = lax.ppermute(rim_own, "seq", [(s, s + 1) for s in range(count - 1)])
    queries = product(mixed_in, w_query)
    key_rows = product(mixed_in, w_key)
    values = product(mixed_in, w_value)
    share = rows * states * width / (256 * 64 * 768)
    shifted, inputs, ends = per_group(
        ends_kernel,
        (key_rows, values, rim, taps, rate),
        ((rows, F32), (rows, F32), (states, F32)),
        [pltpu.VMEM((rows + 8, LANES), F32)],
        4.3 * share,
    )
    strict = len(wires.stages) == 4
    turns = Turns(strict)
    forward = Prefix(turns, ends, rate, rows, False)
    local_made = None
    for groups in thirds(width):
        local_made = per_group(
            mix_kernel,
            (turns.take(inputs), rate, read, skip_row),
            ((rows, F32), (states, F32)),
            [pltpu.VMEM((rows * 8, LANES), F32)],
            11 * share,
            groups,
            local_made,
        )
        turns.give(local_made)
        if forward.done == 0:
            far_grad_out = wires.other_core(turns.take(grad_out))
            far_mixed_in = wires.other_core(turns.take(mixed_in))
        if forward.done < len(forward.bits) - 1:
            forward.step()
    local_mixed, end_ramp = local_made
    all_grad_out = both(turns.take(grad_out), far_grad_out)
    all_mixed_in = both(mixed_in, far_mixed_in)
    turns.give((all_grad_out, all_mixed_in))
    entering = forward.finish()
    mixed, gated = per_group(
        enter_kernel,
        (local_mixed, queries, entering, rate, read),
        ((rows, F32), (rows, BF16)),
        [pltpu.VMEM((rows * 8, LANES), F32)],
        4.5 * share,
    )
    hidden = flat_in + product(gated, w_out)
    ffn_normed, ffn_pull = jax.vjp(layer_norm, hidden, gain_ffn)
    ffn_in = ffn_normed.astype(BF16)
    upper = product(ffn_in, w_up)
    activated, gelu_pull = jax.vjp(gelu_tanh, upper)
    act = activated.astype(BF16)

    turns = Turns(strict)
    sums, made, whole = {}, {"own": None}, {}
    first = wires.core == 0

    def own(value, axis=1):
        return part(value, wires.core, 2, axis)

    def others(value, axis=1):
        return part(value, 1 - wires.core, 2, axis)

    def forward_over():
        sent = others(act)
        turns.give(sent)
        all_act = both(own(act), wires.other_core(sent))
        right = all_grad_out.shape[1] // 2
        sums[0] = Sum(links[0], turns, all_act, all_grad_out[:, :right])
        sums[1] = Sum(links[1], turns, all_act, all_grad_out[:, right:])
        made["ffn_in"] = both(ffn_in, wires.other_core(turns.take(ffn_in)))

    def put_out():
        made["output"] = (hidden + product(turns.take(act), w_down)).astype(BF16)
        turns.give(made["output"])

    def up_back():
        grad_act = back_product(turns.take(grad_out), w_down)
        grad_upper = gelu_pull(grad_act)[0].astype(BF16)
        made["grad_upper"] = grad_upper
        turns.give(grad_upper)
        right = both(own(grad_upper), wires.other_core(others(grad_upper)))
        middle = right.shape[1] // 2
        sums[2] = Sum(links[2], turns, made["ffn_in"], right[:, :middle])
        sums[3] = Sum(links[3], turns, made["ffn_in"], right[:, middle:])

    def branch_back():
        grad_ffn = back_product(turns.take(made["grad_upper"]), w_up)
        grad_hidden_norm, made["d_gain_ffn"] = ffn_pull(grad_ffn)
        made["grad_hidden"] = grad_out.astype(F32) + grad_hidden_norm
        made["grad_branch"] = made["grad_hidden"].astype(BF16)
        made["grad_gated"] = back_product(made["grad_branch"], w_out)
        turns.give(made["grad_gated"])

    def towards():
        made["grad_queries"], made["grad_mixed"], starts = per_group(
            towards_kernel,
            (turns.take(made["grad_gated"]), queries, mixed, rate),
            ((rows, BF16), (rows, F32), (states, F32)),
            [],
            4.8 * share,
        )
        turns.give(starts)
        all_gated = both(gated, wires.other_core(gated))
        sent = jnp.where(first, made["grad_queries"], made["grad_branch"])
        kept = jnp.where(first, made["grad_branch"], made["grad_queries"])
        left = jnp.where(first, all_gated, all_mixed_in)
        sums[4] = Sum(links[4], turns, left, both(kept, wires.other_core(sent)))
        made["prefix"] = Prefix(turns, starts, rate, rows, True)

    def own_back(groups):
        made["own"] = per_group(
            back_kernel,
            (turns.take(made["grad_mixed"]), inputs, rate, read, skip_row),
            ((rows, F32), (states, F32), (states, F32), (states, F32)),
            [pltpu.VMEM((rows * 8, LANES), F32)],
            22 * share,
            groups,
            made["own"],
        )
        turns.give(made["own"])

    def mixer_back():
        adjoint = turns.take(made["prefix"].finish())
        local_grad, *own_sums = made["own"]
        out = per_group(
            adjoint_kernel,
            (
                local_grad,
                made["grad_mixed"],
                inputs,
                shifted,
                values,
                key_rows,
                rim,
                taps,
                rate,
                read,
                entering,
                adjoint,
                ends,
                end_ramp,
                *own_sums,
            ),
            ((rows, BF16), (rows, F32), (8, F32), (states, F32), (states, F32), (states, F32)),
            [pltpu.VMEM((rows * 8, LANES), F32), pltpu.VMEM((rows + 8, LANES), F32)],
            7 * share,
        )
        made["grad_values"], made["grad_keys"], head, *made["small"] = out
        turns.give(head)
        made["behind"] = lax.ppermute(head, "seq", [(s + 1, s) for s in range(count - 1)])

    def rim_back():
        behind, local_keys = turns.take(made["behind"]), made["grad_keys"]
        padded = jnp.concatenate([jnp.zeros_like(behind), behind[:4]], 0)
        late = sum(taps[j] * padded[j : j + 8] for j in range(1, 4))
        made["grad_keys"] = jnp.concatenate(
            [local_keys[: rows - 8], local_keys[rows - 8 :] + late], 0
        ).astype(BF16)
        turns.give(made["grad_keys"])
        sent = jnp.where(first, made["grad_values"], made["grad_keys"])
        kept = jnp.where(first, made["grad_keys"], made["grad_values"])
        made["both"] = both(kept, wires.other_core(sent))

    def input_back():
        grad_normed = (
            back_product(turns.take(made["grad_keys"]), w_key)
            + back_product(made["grad_queries"], w_query)
            + back_product(made["grad_values"], w_value)
        )
        grad_input_norm, made["d_gain_mix"] = norm_pull(grad_normed)
        made["d_tokens"] = (made["grad_hidden"] + grad_input_norm).astype(BF16)
        turns.give(made["d_tokens"])

        totals, slopes, small = made["small"]
        gains = jnp.stack([made["d_gain_mix"], made["d_gain_ffn"]])
        gains = jnp.pad(gains, ((0, states - 2), (0, 0)))
        upper = wires.swap_batch(jnp.where(first, slopes, totals), 1)
        lower = wires.swap_batch(jnp.where(first, gains, small), 1)
        tail = (
            (jnp.where(first, totals, slopes), jnp.where(first, small, gains)),
            (upper, lower),
        )
        sums[5] = Sum(links[5], turns, all_mixed_in, made["both"], tail)

    joins = (
        (w_down.shape, "rows", 0, 0),
        (w_down.shape, "rows", 0, width // 2),
        (w_up.shape, "columns", 0, 0),
        (w_up.shape, "columns", 0, w_up.shape[1] // 4),
        (w_out.shape, "tensors"),
        (w_key.shape, "tensors", states),
    )
    steps = {
        "X": forward_over,
        "O": put_out,
        "G1": up_back,
        "G2": branch_back,
        "K1": towards,
        "P": lambda: made["prefix"].step(),
        "L0": lambda: own_back(thirds(width)[0]),
        "L1": lambda: own_back(thirds(width)[1]),
        "L2": lambda: own_back(thirds(width)[2]),
        "B0": mixer_back,
        "R": rim_back,
        "E": input_back,
    }
    for name in ORDER if strict and ORDER else plain_order(6, len(wires.stages)):
        with jax.named_scope(name):
            if name[0] == "A":
                sums[int(name[-1])].step(int(name[1:-1]))
            elif name[0] == "F":
                sums[int(name[-1])].cross()
            elif name[0] == "J":
                number = int(name[-1])
                into = None
                if number < 4 and number ^ 1 in whole:
                    into = whole[number ^ 1][0]
                whole[number] = sums[number].join(*joins[number], into=into)
            else:
                steps[name]()
    last = list(whole)
    d_down, d_up = (whole[max(pair, key=last.index)][0] for pair in ((0, 1), (2, 3)))
    d_out, d_query = whole[4]
    d_key, d_value, tails = whole[5]
    part_a, part_b = tails[: 2 * states], tails[2 * states :]
    d_tokens = made["d_tokens"].reshape(tokens.shape)
    totals, slopes = part_a[:states], part_b[:states]
    d_scale = gain_c * totals
    d_decay = read * slopes
    root = jnp.sqrt(-jnp.expm1(-2.0 * rate))
    d_rate = -jnp.exp(-rate) * d_decay + d_scale * gain_b * jnp.exp(-2.0 * rate) / root
    return (
        made["output"].reshape(tokens.shape),
        d_tokens,
        d_query,
        d_key,
        d_value,
        d_out,
        d_up,
        d_down,
        part_b[states],
        part_b[states + 1],
        part_a[states : states + 4],
        d_rate,
        d_scale * root,
        scale * totals,
        part_a[states + 4],
    )


def half_columns(value, which):
    columns = value.shape[1] // 2
    return lax.dynamic_slice_in_dim(value, which * columns, columns, 1)


def solution(mesh):
    split = P("batch", "seq", None)
    in_specs = (split,) + (P(),) * 13 + (split,)
    out_specs = (split, split) + (P(),) * 13
    return jax.shard_map(local, mesh=mesh, in_specs=in_specs, out_specs=out_specs, check_vma=False)
```
